32 devices in a mesh: gx: 8 (over y, x, core), gy: 4 (over z).
Axes of the slice: x: 2, y: 2, z: 4, core: 2. Of those that a mesh axis runs over, the one named last changes fastest.
Arguments:
- queries: bfloat16 [1024, 256], P(('gx', 'gy')), may hold values from -32 to 32
- positions: int32 [1024], P(('gx', 'gy')), may hold values from 0 to 16383
- queue: bfloat16 [16384, 256], P('gx'), may hold values from -4 to 4
- new_keys: bfloat16 [2048, 256], P(('gx', 'gy')), may hold values from -4 to 4
- step: int32 [1], replicated, may hold values from 0 to 1023
Outputs:
- losses: float32 [1024], P(('gx', 'gy'))
- query_grad: bfloat16 [1024, 256], P(('gx', 'gy'))
- updated_queue: bfloat16 [16384, 256], P('gx')
The draws below stay inside these ranges and needn't reach their ends.
All inputs are finite; a program needn't handle non-finite values.
Results may differ from the reference program's by a relative error of at most 0.0029.
Values may be sent and summed in bfloat16 or wider, within the bound.
A program may use at most 64 MiB of HBM per device.

```python
import math
import jax
import jax.numpy as jnp
from jax import lax

E = 256
KEY_DEV = 2048
BATCH = 1024
QUEUE = 16384
N_GX = 8


def queue_base(key):
    base = jnp.clip(jax.random.normal(jax.random.fold_in(key, 11), (QUEUE, E), jnp.float32), -4.0, 4.0)
    pairs = base.reshape(QUEUE // 2, 2, E)
    second = pairs[:, 1]
    joined = jnp.stack([pairs[:, 0], second], axis=1).reshape(QUEUE, E)
    return jnp.clip(joined, -4.0, 4.0)


def draw_queue(key, part):
    table = queue_base(key)
    return table.astype(jnp.bfloat16)


def draw_queries(key, part):
    key = jax.random.fold_in(key, 3)
    rows = jnp.clip(jax.random.normal(key, (BATCH, E), jnp.float32), -4.0, 4.0)
    return rows.astype(jnp.bfloat16)


def plant(entries, stream_key, least, top_value):
    spot = [jax.random.randint(jax.random.fold_in(stream_key, axis), (), 0, length) for axis, length in enumerate(entries.shape)]
    main_axis = entries.shape.index(max(entries.shape))
    next_to = spot[:main_axis] + [(spot[main_axis] + 1) % entries.shape[main_axis]] + spot[main_axis + 1:]
    return entries.at[tuple(spot)].set(least).at[tuple(next_to)].set(top_value)


def steps_of(rng, extent, cuts, low, top_value):
    loudness = 1.0
    for dim, blocks in cuts:
        heights = jax.random.uniform(jax.random.fold_in(jax.random.fold_in(rng, 6), dim), (blocks,), jnp.float32, low / len(cuts), top_value / len(cuts))
        loudness = loudness * jnp.repeat(jnp.exp(heights), extent[dim] // blocks).reshape((-1,) + (1,) * (len(extent) - 1 - dim))
    return loudness


def bell_draw(rng, dims, width, bound, shards=(), held_as=jnp.bfloat16):
    gain = steps_of(rng, dims, shards, -0.22, 0.18) if shards else 1.0
    result = jax.random.normal(rng, dims, jnp.float32) * width * gain
    return jnp.minimum(jnp.maximum(result, -bound), bound).astype(held_as)


def setup_inputs(seed: int = 0) -> dict:
    seeds = jax.random.split(jax.random.key(seed), 6)
    return {
        "queries": draw_queries(jax.random.fold_in(seeds[5], 71), 0),
        "positions": plant(jax.random.randint(seeds[1], (BATCH,), 0, QUEUE), jax.random.fold_in(seeds[1], 1), 0, QUEUE - 1).astype(jnp.int32),
        "queue": draw_queue(jax.random.fold_in(seeds[5], 71), 0),
        "new_keys": bell_draw(seeds[3], (KEY_DEV, E), 1.0, 4.0, ((0, 32),)),
        "step": jax.random.randint(seeds[4], (1,), 0, 1024).astype(jnp.int32),
    }


def reference(queries, positions, queue, new_keys, step):
    scale = 2.0 / math.sqrt(E)
    block = math.gcd(BATCH, 256)
    query_blocks = queries.reshape(BATCH // block, block, E)
    pos_blocks = positions.reshape(BATCH // block, block)

    def one_block(pair):
        rows, targets = pair
        scores = jnp.dot(rows, queue.T, preferred_element_type=jnp.float32) * scale
        top = lax.optimization_barrier(jnp.max(scores, axis=1))
        lse = top + jnp.log(lax.optimization_barrier(jnp.sum(jnp.exp(scores - top[:, None]), axis=1)))
        hits = lax.broadcasted_iota(jnp.int32, scores.shape, 1) == targets[:, None]
        positive = lax.optimization_barrier(jnp.sum(jnp.where(hits, scores, 0.0), axis=1))
        weights = (jnp.exp(scores - lse[:, None]) - hits.astype(scores.dtype)).astype(jnp.bfloat16)
        grad = (jnp.dot(weights, queue, preferred_element_type=jnp.float32) * scale).astype(jnp.bfloat16)
        return (lse - positive, grad)
    losses, grads = lax.map(one_block, (query_blocks, pos_blocks))
    owner = step[0] % N_GX
    slabs = queue.reshape(N_GX, KEY_DEV, E)
    chosen = jnp.arange(N_GX, dtype=jnp.int32) == owner
    updated = jnp.where(chosen[:, None, None], new_keys[None], slabs).reshape(QUEUE, E)
    return (losses.reshape(BATCH), grads.reshape(BATCH, E), updated)
```

```python
import functools
import math

import jax
import jax.numpy as jnp
from jax import lax
from jax.experimental import pallas as pl
from jax.experimental.pallas import tpu as pltpu
from jax.sharding import PartitionSpec as P

MESH = pl.DeviceIdType.MESH
LANES = 128
F32 = jnp.float32
BF16 = jnp.bfloat16


def diagonal(rows):
    shape = (rows, LANES)
    return lax.broadcasted_iota(jnp.int32, shape, 0) == lax.broadcasted_iota(jnp.int32, shape, 1)


def to_column(row, diag):
    return jnp.sum(jnp.where(diag, row, 0.0), axis=1, keepdims=True)


def to_row(column, diag):
    return jnp.sum(jnp.where(diag, column, 0.0), axis=0, keepdims=True)


def exchange(
    n, ngy, scale,
    q_ref, pos_ref, queue_ref, nk_ref,
    loss_ref, grad_ref, arrived_ref,
    keys, q_all, p_all, pos_v, part_send, part_recv, stat_send, stat_recv,
    local_sem, q_ss, q_rs, p_ss, p_rs, z_ss, z_rs, k_ss, f_ss, k_rs, g_ss, g_rs, s_ss, s_rs,
):
    i = lax.axis_index("gx")
    j = lax.axis_index("gy")
    q_dev, width = q_ref.shape
    key_dev = queue_ref.shape[0]

    def send(src, dst, ss, rs, to):
        return pltpu.make_async_remote_copy(
            src_ref=src, dst_ref=dst, send_sem=ss, recv_sem=rs, device_id=to, device_id_type=MESH
        )

    def gx_peers(body):
        for d in range(1, n):
            body(lax.rem(i + d, n))

    def gy_peers(body):
        for d in range(1, ngy):
            body(lax.rem(j + d, ngy))

    load_pos = pltpu.make_async_copy(pos_ref, pos_v, local_sem.at[0])
    load_q = pltpu.make_async_copy(q_ref, q_all.at[i], local_sem.at[1])
    load_keys = pltpu.make_async_copy(queue_ref, keys, local_sem.at[2])
    own_new = pltpu.make_async_copy(nk_ref, arrived_ref.at[i * ngy + j], local_sem.at[3])
    load_pos.start()
    load_q.start()
    load_keys.start()
    own_new.start()

    barrier = pltpu.get_barrier_semaphore()
    gx_peers(lambda p: pl.semaphore_signal(barrier, inc=1, device_id=(p, j), device_id_type=MESH))
    gy_peers(lambda p: pl.semaphore_signal(barrier, inc=1, device_id=(i, p), device_id_type=MESH))
    load_pos.wait()
    load_q.wait()
    diag = diagonal(q_dev)
    p_all[i] = jnp.zeros((1, LANES), jnp.int32)
    p_all[i, :, 0:q_dev] = pos_v[...].reshape(1, q_dev)
    pl.semaphore_wait(barrier, n + ngy - 2)

    def q_copy(p):
        return send(q_all.at[i], q_all.at[i], q_ss.at[p], q_rs.at[i], (p, j))

    def p_copy(p):
        return send(p_all.at[i], p_all.at[i], p_ss.at[p], p_rs.at[i], (p, j))

    def start_queries(p):
        p_copy(p).start()
        q_copy(p).start()

    gx_peers(start_queries)

    def z_copy(p):
        return send(nk_ref, arrived_ref.at[i * ngy + j], z_ss.at[p], z_rs.at[j], (i, p))

    gy_peers(lambda p: z_copy(p).start())

    def wait_in(dst, sem):
        pltpu.make_async_copy(dst, dst, sem).wait()

    partner = i + 1 - 2 * lax.rem(i, 2)

    def rows_of(k):
        return arrived_ref.at[pl.ds(k * ngy, ngy)]

    def k_copy(p):
        return send(rows_of(i), rows_of(i), k_ss.at[p], k_rs.at[i], (p, j))

    def f_copy(k):
        return send(rows_of(k), rows_of(k), f_ss.at[k], k_rs.at[k], (partner, j))

    def same_core(body):
        for d in range(2, n, 2):
            body(lax.rem(i + d, n))

    load_keys.wait()

    def wait_queries(p):
        wait_in(p_all.at[p], p_rs.at[p])
        wait_in(q_all.at[p], q_rs.at[p])

    gx_peers(wait_queries)

    own_new.wait()
    gy_peers(lambda p: wait_in(arrived_ref.at[i * ngy + p], z_rs.at[p]))
    same_core(lambda p: k_copy(p).start())
    k_copy(partner).start()

    group = min(n, 256 // q_dev)
    rows = group * q_dev

    def work(c):
        at = c * group
        columns = [to_column(p_all[at + b].astype(F32), diag) for b in range(group)]
        target = jnp.concatenate(columns, axis=0).astype(jnp.int32) - i * key_dev
        q = q_all[pl.ds(at, group)].reshape(rows, width)
        slab = keys[...]
        scores = lax.dot_general(q, slab, (((1,), (1,)), ((), ())), preferred_element_type=F32) * scale
        hits = lax.broadcasted_iota(jnp.int32, scores.shape, 1) == target
        top = jnp.max(scores, axis=1, keepdims=True)
        positive = jnp.sum(jnp.where(hits, scores, 0.0), axis=1, keepdims=True)
        powers = jnp.exp(scores - top)
        total = jnp.sum(powers, axis=1, keepdims=True)
        others = jnp.where(hits, 0.0, powers).astype(BF16)
        part = jnp.dot(others, slab, preferred_element_type=F32)
        row = jnp.dot(hits.astype(F32).astype(BF16), slab, preferred_element_type=F32)
        high = part.astype(BF16)
        low = part - high.astype(F32)
        inside = jnp.logical_and(target >= 0, target < key_dev)
        second = jnp.where(inside, row, low).astype(BF16)
        part_send[pl.ds(at, group), 0] = high.reshape(group, q_dev, width)
        part_send[pl.ds(at, group), 1] = second.reshape(group, q_dev, width)
        for b in range(group):
            span = slice(b * q_dev, (b + 1) * q_dev)
            stat_send[at + b, 0:1] = to_row(top[span], diag)
            stat_send[at + b, 1:2] = to_row(total[span], diag)
            stat_send[at + b, 2:3] = to_row(positive[span], diag)
            stat_send[at + b, 3:4] = jnp.zeros((1, LANES), F32)

    if n == group:
        work(0)
    else:
        pl.loop(0, n // group)(work)

    def g_copy(p):
        return send(part_send.at[p], part_recv.at[i], g_ss.at[p], g_rs.at[i], (p, j))

    def s_copy(p):
        return send(stat_send.at[p], stat_recv.at[i], s_ss.at[p], s_rs.at[i], (p, j))

    def start_parts(p):
        s_copy(p).start()
        g_copy(p).start()

    gx_peers(start_parts)
    part_recv[i] = part_send[i]
    stat_recv[i] = stat_send[i]

    def pass_on(k):
        wait_in(rows_of(k), k_rs.at[k])
        f_copy(k).start()

    same_core(pass_on)

    gx_peers(lambda p: wait_in(stat_recv.at[p], s_rs.at[p]))
    top = stat_recv[0, 0:1]
    for s in range(1, n):
        top = jnp.maximum(top, stat_recv[s, 0:1])
    total = jnp.zeros_like(top)
    positive = jnp.zeros_like(top)
    for s in range(n):
        total = total + stat_recv[s, 1:2] * jnp.exp(stat_recv[s, 0:1] - top)
        positive = positive + stat_recv[s, 2:3]
    lse = top + jnp.log(total)
    loss_ref[...] = lse - positive
    own = to_column(p_all[i].astype(F32), diag).astype(jnp.int32)
    at_positive = to_column(jnp.exp(positive - lse) - 1.0, diag)
    factors = [to_column(jnp.exp(stat_recv[s, 0:1] - lse), diag) for s in range(n)]

    gx_peers(lambda p: wait_in(part_recv.at[p], g_rs.at[p]))
    grad = jnp.zeros((q_dev, width), F32)
    for s in range(n):
        first = part_recv[s, 0].astype(F32)
        second = part_recv[s, 1].astype(F32)
        inside = jnp.logical_and(own >= s * key_dev, own < (s + 1) * key_dev)
        grad = grad + factors[s] * first + jnp.where(inside, at_positive, factors[s]) * second
    grad_ref[...] = (grad * scale).astype(BF16)

    wait_in(rows_of(partner), k_rs.at[partner])
    for d in range(2, n, 2):
        k = lax.rem(partner + d, n)
        wait_in(rows_of(k), k_rs.at[k])

    def end_sends(p):
        p_copy(p).wait_send()
        q_copy(p).wait_send()
        s_copy(p).wait_send()
        g_copy(p).wait_send()

    gx_peers(end_sends)
    gy_peers(lambda p: z_copy(p).wait_send())
    same_core(lambda p: k_copy(p).wait_send())
    k_copy(partner).wait_send()
    same_core(lambda k: f_copy(k).wait_send())


def finish(
    n, step_ref, loss_ref, grad_ref, queue_ref, arrived_ref, loss_out, grad_out, updated_ref, sem
):
    here = lax.rem(step_ref[0], n) == lax.axis_index("gx")

    @pl.when(here)
    def _():
        pltpu.make_async_copy(arrived_ref, updated_ref, sem.at[0]).start()

    @pl.when(jnp.logical_not(here))
    def _():
        pltpu.make_async_copy(queue_ref, updated_ref, sem.at[0]).start()

    loss_out[...] = loss_ref[0, 0 : loss_out.shape[0]]
    grad_out[...] = grad_ref[...]
    pltpu.make_async_copy(queue_ref, updated_ref, sem.at[0]).wait()


def local(n, ngy, queries, positions, queue, new_keys, step):
    q_dev, width = queries.shape
    key_dev = queue.shape[0]
    nk_dev = new_keys.shape[0]
    scale = 2.0 / math.sqrt(width)
    anywhere = pl.BlockSpec(memory_space=pl.ANY)
    vmem = pl.BlockSpec(memory_space=pltpu.VMEM)
    dma = pltpu.SemaphoreType.DMA
    rows = n * q_dev
    loss_row, grad, arrived = pl.pallas_call(
        functools.partial(exchange, n, ngy, scale),
        out_shape=(
            jax.ShapeDtypeStruct((1, LANES), F32),
            jax.ShapeDtypeStruct((q_dev, width), BF16),
            jax.ShapeDtypeStruct((n * ngy, nk_dev, width), BF16),
        ),
        in_specs=[anywhere] * 4,
        out_specs=(vmem, vmem, anywhere),
        scratch_shapes=[
            pltpu.VMEM((key_dev, width), BF16),
            pltpu.VMEM((n, q_dev, width), BF16),
            pltpu.VMEM((n, 1, LANES), jnp.int32),
            pltpu.VMEM((q_dev,), jnp.int32),
            pltpu.VMEM((n, 2, q_dev, width), BF16),
            pltpu.VMEM((n, 2, q_dev, width), BF16),
            pltpu.VMEM((n, 4, LANES), F32),
            pltpu.VMEM((n, 4, LANES), F32),
            dma((4,)),
            dma((n,)), dma((n,)), dma((n,)), dma((n,)),
            dma((ngy,)), dma((ngy,)),
            dma((n,)), dma((n,)), dma((n,)),
            dma((n,)), dma((n,)), dma((n,)), dma((n,)),
        ],
        compiler_params=pltpu.CompilerParams(
            collective_id=0, has_side_effects=True, vmem_limit_bytes=48 * 2**20
        ),
        cost_estimate=pl.CostEstimate(
            flops=6 * rows * key_dev * width,
            bytes_accessed=2 * key_dev * width * 2,
            transcendentals=rows * key_dev,
        ),
        name="exchange",
    )(queries, positions, queue, new_keys)
    return pl.pallas_call(
        functools.partial(finish, n),
        out_shape=(
            jax.ShapeDtypeStruct((q_dev,), F32),
            jax.ShapeDtypeStruct((q_dev, width), BF16),
            jax.ShapeDtypeStruct((key_dev, width), BF16),
        ),
        in_specs=[pl.BlockSpec(memory_space=pltpu.SMEM), vmem, vmem, anywhere, anywhere],
        out_specs=(vmem, vmem, anywhere),
        scratch_shapes=[dma((1,))],
        name="finish",
    )(step, loss_row, grad, queue, arrived.reshape(key_dev, width))


def solution(mesh):
    return jax.shard_map(
        functools.partial(local, mesh.shape["gx"], mesh.shape["gy"]),
        mesh=mesh,
        in_specs=(
            P(("gx", "gy"), None),
            P(("gx", "gy")),
            P("gx", None),
            P(("gx", "gy"), None),
            P(),
        ),
        out_specs=(P(("gx", "gy")), P(("gx", "gy"), None), P("gx", None)),
        check_vma=False,
    )
```

```python
import functools
import math

import jax
import jax.numpy as jnp
from jax import lax
from jax.experimental import pallas as pl
from jax.experimental.pallas import tpu as pltpu
from jax.sharding import PartitionSpec as P

MESH = pl.DeviceIdType.MESH
LANES = 128
F32 = jnp.float32
BF16 = jnp.bfloat16


def diagonal(rows):
    shape = (rows, LANES)
    return lax.broadcasted_iota(jnp.int32, shape, 0) == lax.broadcasted_iota(jnp.int32, shape, 1)


def to_column(row, diag):
    return jnp.sum(jnp.where(diag, row, 0.0), axis=1, keepdims=True)


def to_row(column, diag):
    return jnp.sum(jnp.where(diag, column, 0.0), axis=0, keepdims=True)


def exchange(
    n, ngy, scale,
    q_ref, pos_ref, queue_ref, nk_ref,
    loss_ref, grad_ref, gathered_ref,
    arrived_ref, keep_sem, keys, q_all, p_all, pos_v, part_send, part_recv, stat_send, stat_recv,
    local_sem, q_ss, q_rs, p_ss, p_rs, z_ss, z_rs, k_ss, f_ss, k_rs, g_ss, g_rs, s_ss, s_rs,
):
    i = lax.axis_index("gx")
    j = lax.axis_index("gy")
    q_dev, width = q_ref.shape
    key_dev = queue_ref.shape[0]

    def send(src, dst, ss, rs, to):
        return pltpu.make_async_remote_copy(
            src_ref=src, dst_ref=dst, send_sem=ss, recv_sem=rs, device_id=to, device_id_type=MESH
        )

    def gx_peers(body):
        for d in range(1, n):
            body(lax.rem(i + d, n))

    def gy_peers(body):
        for d in range(1, ngy):
            body(lax.rem(j + d, ngy))

    load_pos = pltpu.make_async_copy(pos_ref, pos_v, local_sem.at[0])
    load_q = pltpu.make_async_copy(q_ref, q_all.at[i], local_sem.at[1])
    load_keys = pltpu.make_async_copy(queue_ref, keys, local_sem.at[2])
    own_new = pltpu.make_async_copy(nk_ref, arrived_ref.at[i * ngy + j], local_sem.at[3])
    load_pos.start()
    load_q.start()
    load_keys.start()
    own_new.start()

    barrier = pltpu.get_barrier_semaphore()
    gx_peers(lambda p: pl.semaphore_signal(barrier, inc=1, device_id=(p, j), device_id_type=MESH))
    gy_peers(lambda p: pl.semaphore_signal(barrier, inc=1, device_id=(i, p), device_id_type=MESH))
    load_pos.wait()
    load_q.wait()
    diag = diagonal(q_dev)
    p_all[i] = jnp.zeros((1, LANES), jnp.int32)
    p_all[i, :, 0:q_dev] = pos_v[...].reshape(1, q_dev)
    pl.semaphore_wait(barrier, n + ngy - 2)

    def q_copy(p):
        return send(q_all.at[i], q_all.at[i], q_ss.at[p], q_rs.at[i], (p, j))

    def p_copy(p):
        return send(p_all.at[i], p_all.at[i], p_ss.at[p], p_rs.at[i], (p, j))

    def start_queries(p):
        p_copy(p).start()
        q_copy(p).start()

    gx_peers(start_queries)

    def z_copy(p):
        return send(arrived_ref.at[i * ngy + j], arrived_ref.at[i * ngy + j], z_ss.at[p], z_rs.at[j], (i, p))

    own_new.wait()
    gy_peers(lambda p: z_copy(p).start())

    def wait_in(dst, sem):
        pltpu.make_async_copy(dst, dst, sem).wait()

    partner = i + 1 - 2 * lax.rem(i, 2)

    def rows_of(k):
        return arrived_ref.at[pl.ds(k * ngy, ngy)]

    def k_copy(p):
        return send(rows_of(i), rows_of(i), k_ss.at[p], k_rs.at[i], (p, j))

    def f_copy(k):
        return send(rows_of(k), rows_of(k), f_ss.at[k], k_rs.at[k], (partner, j))

    def same_core(body):
        for d in range(2, n, 2):
            body(lax.rem(i + d, n))

    load_keys.wait()

    def wait_queries(p):
        wait_in(p_all.at[p], p_rs.at[p])
        wait_in(q_all.at[p], q_rs.at[p])

    gx_peers(wait_queries)

    gy_peers(lambda p: wait_in(arrived_ref.at[i * ngy + p], z_rs.at[p]))
    same_core(lambda p: k_copy(p).start())
    k_copy(partner).start()

    def keep(k):
        return pltpu.make_async_copy(rows_of(k), gathered_ref.at[pl.ds(k * ngy, ngy)], keep_sem.at[k])

    keep(i).start()

    group = min(n, 256 // q_dev)
    rows = group * q_dev

    def work(c):
        at = c * group
        columns = [to_column(p_all[at + b].astype(F32), diag) for b in range(group)]
        target = jnp.concatenate(columns, axis=0).astype(jnp.int32) - i * key_dev
        q = q_all[pl.ds(at, group)].reshape(rows, width)
        slab = keys[...]
        scores = lax.dot_general(q, slab, (((1,), (1,)), ((), ())), preferred_element_type=F32) * scale
        hits = lax.broadcasted_iota(jnp.int32, scores.shape, 1) == target
        top = jnp.max(scores, axis=1, keepdims=True)
        positive = jnp.sum(jnp.where(hits, scores, 0.0), axis=1, keepdims=True)
        powers = jnp.exp(scores - top)
        total = jnp.sum(powers, axis=1, keepdims=True)
        others = jnp.where(hits, 0.0, powers).astype(BF16)
        part = jnp.dot(others, slab, preferred_element_type=F32)
        row = jnp.dot(hits.astype(F32).astype(BF16), slab, preferred_element_type=F32)
        high = part.astype(BF16)
        low = part - high.astype(F32)
        inside = jnp.logical_and(target >= 0, target < key_dev)
        second = jnp.where(inside, row, low).astype(BF16)
        part_send[pl.ds(at, group), 0] = high.reshape(group, q_dev, width)
        part_send[pl.ds(at, group), 1] = second.reshape(group, q_dev, width)
        for b in range(group):
            span = slice(b * q_dev, (b + 1) * q_dev)
            stat_send[at + b, 0:1] = to_row(top[span], diag)
            stat_send[at + b, 1:2] = to_row(total[span], diag)
            stat_send[at + b, 2:3] = to_row(positive[span], diag)
            stat_send[at + b, 3:4] = jnp.zeros((1, LANES), F32)

    if n == group:
        work(0)
    else:
        pl.loop(0, n // group)(work)

    def g_copy(p):
        return send(part_send.at[p], part_recv.at[i], g_ss.at[p], g_rs.at[i], (p, j))

    def s_copy(p):
        return send(stat_send.at[p], stat_recv.at[i], s_ss.at[p], s_rs.at[i], (p, j))

    def start_parts(p):
        s_copy(p).start()
        g_copy(p).start()

    gx_peers(start_parts)
    part_recv[i] = part_send[i]
    stat_recv[i] = stat_send[i]

    def pass_on(k):
        wait_in(rows_of(k), k_rs.at[k])
        f_copy(k).start()
        keep(k).start()

    same_core(pass_on)

    gx_peers(lambda p: wait_in(stat_recv.at[p], s_rs.at[p]))
    top = stat_recv[0, 0:1]
    for s in range(1, n):
        top = jnp.maximum(top, stat_recv[s, 0:1])
    total = jnp.zeros_like(top)
    positive = jnp.zeros_like(top)
    for s in range(n):
        total = total + stat_recv[s, 1:2] * jnp.exp(stat_recv[s, 0:1] - top)
        positive = positive + stat_recv[s, 2:3]
    lse = top + jnp.log(total)
    loss_ref[...] = lse - positive
    own = to_column(p_all[i].astype(F32), diag).astype(jnp.int32)
    at_positive = to_column(jnp.exp(positive - lse) - 1.0, diag)
    factors = [to_column(jnp.exp(stat_recv[s, 0:1] - lse), diag) for s in range(n)]

    gx_peers(lambda p: wait_in(part_recv.at[p], g_rs.at[p]))
    grad = jnp.zeros((q_dev, width), F32)
    for s in range(n):
        first = part_recv[s, 0].astype(F32)
        second = part_recv[s, 1].astype(F32)
        inside = jnp.logical_and(own >= s * key_dev, own < (s + 1) * key_dev)
        grad = grad + factors[s] * first + jnp.where(inside, at_positive, factors[s]) * second
    grad_ref[...] = (grad * scale).astype(BF16)

    for d in range(0, n, 2):
        k = lax.rem(partner + d, n)
        wait_in(rows_of(k), k_rs.at[k])
        keep(k).start()

    def end_sends(p):
        p_copy(p).wait_send()
        q_copy(p).wait_send()
        s_copy(p).wait_send()
        g_copy(p).wait_send()

    gx_peers(end_sends)
    gy_peers(lambda p: z_copy(p).wait_send())
    same_core(lambda p: k_copy(p).wait_send())
    k_copy(partner).wait_send()
    same_core(lambda k: f_copy(k).wait_send())
    for k in range(n):
        keep(k).wait()


def finish(
    n, step_ref, loss_ref, grad_ref, queue_ref, arrived_ref, loss_out, grad_out, updated_ref,
    loss_v, loss_w, grad_v, slab, in_sem, out_sem, small_in, small_out,
):
    here = lax.rem(step_ref[0], n) == lax.axis_index("gx")
    pieces = in_sem.shape[0]
    size = slab.shape[0] // pieces

    def part(c):
        return pl.ds(c * size, size)

    def load(src, c):
        return pltpu.make_async_copy(src.at[part(c)], slab.at[part(c)], in_sem.at[c])

    def store(c):
        return pltpu.make_async_copy(slab.at[part(c)], updated_ref.at[part(c)], out_sem.at[c])

    @pl.when(here)
    def _():
        for c in range(pieces):
            load(arrived_ref, c).start()

    @pl.when(jnp.logical_not(here))
    def _():
        for c in range(pieces):
            load(queue_ref, c).start()

    loss_load = pltpu.make_async_copy(loss_ref, loss_v, small_in.at[0])
    grad_load = pltpu.make_async_copy(grad_ref, grad_v, small_in.at[1])
    loss_store = pltpu.make_async_copy(loss_w, loss_out, small_out.at[0])
    grad_store = pltpu.make_async_copy(grad_v, grad_out, small_out.at[1])
    loss_load.start()
    grad_load.start()
    for c in range(pieces):
        load(queue_ref, c).wait()
        store(c).start()
    loss_load.wait()
    loss_w[...] = loss_v[0, 0 : loss_w.shape[0]]
    loss_store.start()
    grad_load.wait()
    grad_store.start()
    for c in range(pieces):
        store(c).wait()
    loss_store.wait()
    grad_store.wait()


def local(n, ngy, queries, positions, queue, new_keys, step):
    q_dev, width = queries.shape
    key_dev = queue.shape[0]
    nk_dev = new_keys.shape[0]
    scale = 2.0 / math.sqrt(width)
    anywhere = pl.BlockSpec(memory_space=pl.ANY)
    vmem = pl.BlockSpec(memory_space=pltpu.VMEM)
    dma = pltpu.SemaphoreType.DMA
    rows = n * q_dev
    loss_row, grad, arrived = pl.pallas_call(
        functools.partial(exchange, n, ngy, scale),
        out_shape=(
            jax.ShapeDtypeStruct((1, LANES), F32),
            jax.ShapeDtypeStruct((q_dev, width), BF16),
            jax.ShapeDtypeStruct((n * ngy, nk_dev, width), BF16),
        ),
        in_specs=[anywhere] * 4,
        out_specs=(vmem, vmem, anywhere),
        scratch_shapes=[
            pltpu.VMEM((n * ngy, nk_dev, width), BF16),
            dma((n,)),
            pltpu.VMEM((key_dev, width), BF16),
            pltpu.VMEM((n, q_dev, width), BF16),
            pltpu.VMEM((n, 1, LANES), jnp.int32),
            pltpu.VMEM((q_dev,), jnp.int32),
            pltpu.VMEM((n, 2, q_dev, width), BF16),
            pltpu.VMEM((n, 2, q_dev, width), BF16),
            pltpu.VMEM((n, 4, LANES), F32),
            pltpu.VMEM((n, 4, LANES), F32),
            dma((4,)),
            dma((n,)), dma((n,)), dma((n,)), dma((n,)),
            dma((ngy,)), dma((ngy,)),
            dma((n,)), dma((n,)), dma((n,)),
            dma((n,)), dma((n,)), dma((n,)), dma((n,)),
        ],
        compiler_params=pltpu.CompilerParams(
            collective_id=0, has_side_effects=True, vmem_limit_bytes=62 * 2**20
        ),
        cost_estimate=pl.CostEstimate(
            flops=6 * rows * key_dev * width,
            bytes_accessed=2 * key_dev * width * 2,
            transcendentals=rows * key_dev,
        ),
        name="exchange",
    )(queries, positions, queue, new_keys)
    return pl.pallas_call(
        functools.partial(finish, n),
        out_shape=(
            jax.ShapeDtypeStruct((q_dev,), F32),
            jax.ShapeDtypeStruct((q_dev, width), BF16),
            jax.ShapeDtypeStruct((key_dev, width), BF16),
        ),
        in_specs=[pl.BlockSpec(memory_space=pltpu.SMEM)] + [anywhere] * 4,
        out_specs=(anywhere,) * 3,
        scratch_shapes=[
            pltpu.VMEM((1, LANES), F32),
            pltpu.VMEM((q_dev,), F32),
            pltpu.VMEM((q_dev, width), BF16),
            pltpu.VMEM((key_dev, width), BF16),
            dma((8,)),
            dma((8,)),
            dma((2,)),
            dma((2,)),
        ],
        compiler_params=pltpu.CompilerParams(vmem_limit_bytes=62 * 2**20),
        name="finish",
    )(step, loss_row, grad, queue, arrived.reshape(key_dev, width))


def solution(mesh):
    return jax.shard_map(
        functools.partial(local, mesh.shape["gx"], mesh.shape["gy"]),
        mesh=mesh,
        in_specs=(
            P(("gx", "gy"), None),
            P(("gx", "gy")),
            P("gx", None),
            P(("gx", "gy"), None),
            P(),
        ),
        out_specs=(P(("gx", "gy")), P(("gx", "gy"), None), P("gx", None)),
        check_vma=False,
    )
```

```python
import functools
import math

import jax
import jax.numpy as jnp
from jax import lax
from jax.experimental import pallas as pl
from jax.experimental.pallas import tpu as pltpu
from jax.sharding import PartitionSpec as P

MESH = pl.DeviceIdType.MESH
LANES = 128
F32 = jnp.float32
BF16 = jnp.bfloat16


def diagonal(rows):
    shape = (rows, LANES)
    return lax.broadcasted_iota(jnp.int32, shape, 0) == lax.broadcasted_iota(jnp.int32, shape, 1)


def to_column(row, diag):
    return jnp.sum(jnp.where(diag, row, 0.0), axis=1, keepdims=True)


def to_row(column, diag):
    return jnp.sum(jnp.where(diag, column, 0.0), axis=0, keepdims=True)


def exchange(
    n, ngy, scale,
    q_ref, pos_ref, queue_ref, nk_ref,
    loss_ref, grad_ref, gathered_ref,
    arrived_ref, keep_sem, keys, q_all, p_all, pos_v, part_send, part_recv, stat_send, stat_recv,
    local_sem, q_ss, q_rs, p_ss, p_rs, z_ss, z_rs, k_ss, k_rs, r_ss, f_ss, f_rs, g_ss, g_rs, s_ss, s_rs,
):
    i = lax.axis_index("gx")
    j = lax.axis_index("gy")
    q_dev, width = q_ref.shape
    key_dev = queue_ref.shape[0]

    def send(src, dst, ss, rs, to):
        return pltpu.make_async_remote_copy(
            src_ref=src, dst_ref=dst, send_sem=ss, recv_sem=rs, device_id=to, device_id_type=MESH
        )

    def gx_peers(body):
        for d in range(1, n):
            body(lax.rem(i + d, n))

    def gy_peers(body):
        for d in range(1, ngy):
            body(lax.rem(j + d, ngy))

    load_pos = pltpu.make_async_copy(pos_ref, pos_v, local_sem.at[0])
    load_q = pltpu.make_async_copy(q_ref, q_all.at[i], local_sem.at[1])
    load_keys = pltpu.make_async_copy(queue_ref, keys, local_sem.at[2])
    own_new = pltpu.make_async_copy(nk_ref, arrived_ref.at[i * ngy + j], local_sem.at[3])
    load_pos.start()
    load_q.start()
    load_keys.start()
    own_new.start()

    barrier = pltpu.get_barrier_semaphore()
    gx_peers(lambda p: pl.semaphore_signal(barrier, inc=1, device_id=(p, j), device_id_type=MESH))
    gy_peers(lambda p: pl.semaphore_signal(barrier, inc=1, device_id=(i, p), device_id_type=MESH))
    load_pos.wait()
    load_q.wait()
    diag = diagonal(q_dev)
    p_all[i] = jnp.zeros((1, LANES), jnp.int32)
    p_all[i, :, 0:q_dev] = pos_v[...].reshape(1, q_dev)
    pl.semaphore_wait(barrier, n + ngy - 2)

    def q_copy(p):
        return send(q_all.at[i], q_all.at[i], q_ss.at[p], q_rs.at[i], (p, j))

    def p_copy(p):
        return send(p_all.at[i], p_all.at[i], p_ss.at[p], p_rs.at[i], (p, j))

    def start_queries(p):
        p_copy(p).start()
        q_copy(p).start()

    gx_peers(start_queries)

    square = n == 8
    core = lax.rem(i, 2)
    chip = i // 2
    partner = i + 1 - 2 * core
    low_bit, high_bit = lax.rem(chip, 2), chip // 2
    side_a = (high_bit * 2 + 1 - low_bit) * 2 + core
    side_b = ((1 - high_bit) * 2 + low_bit) * 2 + core

    def wait_in(dst, sem):
        pltpu.make_async_copy(dst, dst, sem).wait()

    def block(k, z):
        return arrived_ref.at[k * ngy + z]

    def rows_of(k):
        return arrived_ref.at[pl.ds(k * ngy, ngy)]

    def z_copy(p):
        return send(block(i, j), block(i, j), z_ss.at[p], z_rs.at[j], (i, p))

    def side_copy(z, side, to):
        return send(block(i, z), block(i, z), k_ss.at[side * ngy + z], k_rs.at[i * ngy + z], (to, j))

    def relay_copy(z):
        k, to = (side_a, side_b) if z % 2 == 0 else (side_b, side_a)
        return send(block(k, z), block(k, z), r_ss.at[z], k_rs.at[k * ngy + z], (to, j))

    def k_copy(p):
        return send(rows_of(i), rows_of(i), k_ss.at[p], k_rs.at[i], (p, j))

    def f_copy(k):
        return send(rows_of(k), rows_of(k), f_ss.at[k], f_rs.at[k], (partner, j))

    def keep(k):
        return pltpu.make_async_copy(rows_of(k), gathered_ref.at[pl.ds(k * ngy, ngy)], keep_sem.at[k])

    def same_core(body):
        for d in range(2, n, 2):
            body(lax.rem(i + d, n))

    def to_sides(z):
        side_copy(z, 0, side_a).start()
        side_copy(z, 1, side_b).start()

    own_new.wait()
    gy_peers(lambda p: z_copy(p).start())
    if square:
        to_sides(j)

    def wait_queries(p):
        wait_in(p_all.at[p], p_rs.at[p])
        wait_in(q_all.at[p], q_rs.at[p])

    gx_peers(wait_queries)
    load_keys.wait()

    def next_block(z):
        wait_in(block(i, z), z_rs.at[z])
        if square:
            to_sides(z)

    gy_peers(next_block)
    if not square:
        same_core(lambda p: k_copy(p).start())
    f_copy(i).start()
    keep(i).start()

    group = n // 2 if square else min(n, 256 // q_dev)
    rows = group * q_dev

    def work(at):
        columns = [to_column(p_all[at + b].astype(F32), diag) for b in range(group)]
        target = jnp.concatenate(columns, axis=0).astype(jnp.int32) - i * key_dev
        q = q_all[pl.ds(at, group)].reshape(rows, width)
        slab = keys[...]
        scores = lax.dot_general(q, slab, (((1,), (1,)), ((), ())), preferred_element_type=F32) * scale
        hits = lax.broadcasted_iota(jnp.int32, scores.shape, 1) == target
        top = jnp.max(scores, axis=1, keepdims=True)
        powers = jnp.exp(scores - top)
        total = jnp.sum(powers, axis=1, keepdims=True)
        others = jnp.where(hits, 0.0, powers).astype(BF16)
        part = jnp.dot(others, slab, preferred_element_type=F32)
        row = jnp.dot(hits.astype(F32).astype(BF16), slab, preferred_element_type=F32)
        positive = jnp.sum(q.astype(F32) * row, axis=1, keepdims=True) * scale
        high = part.astype(BF16)
        low = part - high.astype(F32)
        inside = jnp.logical_and(target >= 0, target < key_dev)
        second = jnp.where(inside, row, low).astype(BF16)
        part_send[pl.ds(at, group), 0] = high.reshape(group, q_dev, width)
        part_send[pl.ds(at, group), 1] = second.reshape(group, q_dev, width)
        for b in range(group):
            span = slice(b * q_dev, (b + 1) * q_dev)
            stat_send[at + b, 0:1] = to_row(top[span], diag)
            stat_send[at + b, 1:2] = to_row(total[span], diag)
            stat_send[at + b, 2:3] = to_row(positive[span], diag)
            stat_send[at + b, 3:4] = jnp.zeros((1, LANES), F32)

    def g_copy(p):
        return send(part_send.at[p], part_recv.at[i], g_ss.at[p], g_rs.at[i], (p, j))

    def s_copy(p):
        return send(stat_send.at[p], stat_recv.at[i], s_ss.at[p], s_rs.at[i], (p, j))

    def start_parts(p):
        s_copy(p).start()
        g_copy(p).start()

    if square:
        far = (1 - high_bit) * group
        work(far)
        for b in range(group):
            start_parts(far + b)
        for z in range(ngy):
            k = side_a if z % 2 == 0 else side_b
            wait_in(block(k, z), k_rs.at[k * ngy + z])
            relay_copy(z).start()
        near = high_bit * group
        work(near)
        for d in range(1, group):
            start_parts(near + lax.rem(i - near + d, group))
    else:
        pl.loop(0, n // group)(lambda c: work(c * group))
        gx_peers(start_parts)
    part_recv[i] = part_send[i]
    stat_recv[i] = stat_send[i]

    def pass_on(k):
        f_copy(k).start()
        keep(k).start()

    if square:
        across = 6 - 2 * chip + core
        for z in range(ngy):
            k = side_b if z % 2 == 0 else side_a
            wait_in(block(k, z), k_rs.at[k * ngy + z])
        pass_on(side_a)
        pass_on(side_b)
        for z in range(ngy):
            wait_in(block(across, z), k_rs.at[across * ngy + z])
        pass_on(across)
    else:
        def receive(k):
            wait_in(rows_of(k), k_rs.at[k])
            pass_on(k)

        same_core(receive)

    gx_peers(lambda p: wait_in(stat_recv.at[p], s_rs.at[p]))
    top = stat_recv[0, 0:1]
    for s in range(1, n):
        top = jnp.maximum(top, stat_recv[s, 0:1])
    total = jnp.zeros_like(top)
    positive = jnp.zeros_like(top)
    for s in range(n):
        total = total + stat_recv[s, 1:2] * jnp.exp(stat_recv[s, 0:1] - top)
        positive = positive + stat_recv[s, 2:3]
    lse = top + jnp.log(total)
    loss_ref[...] = lse - positive
    own = to_column(p_all[i].astype(F32), diag).astype(jnp.int32)
    at_positive = to_column(jnp.exp(positive - lse) - 1.0, diag)
    factors = [to_column(jnp.exp(stat_recv[s, 0:1] - lse), diag) for s in range(n)]

    gx_peers(lambda p: wait_in(part_recv.at[p], g_rs.at[p]))
    grad = jnp.zeros((q_dev, width), F32)
    for s in range(n):
        first = part_recv[s, 0].astype(F32)
        second = part_recv[s, 1].astype(F32)
        inside = jnp.logical_and(own >= s * key_dev, own < (s + 1) * key_dev)
        grad = grad + factors[s] * first + jnp.where(inside, at_positive, factors[s]) * second
    grad_ref[...] = (grad * scale).astype(BF16)

    for d in range(0, n, 2):
        k = lax.rem(partner + d, n)
        wait_in(rows_of(k), f_rs.at[k])
        keep(k).start()

    def end_sends(p):
        p_copy(p).wait_send()
        q_copy(p).wait_send()
        s_copy(p).wait_send()
        g_copy(p).wait_send()

    gx_peers(end_sends)
    gy_peers(lambda p: z_copy(p).wait_send())
    if square:
        for z in range(ngy):
            side_copy(z, 0, side_a).wait_send()
            side_copy(z, 1, side_b).wait_send()
            relay_copy(z).wait_send()
    else:
        same_core(lambda p: k_copy(p).wait_send())
    f_copy(i).wait_send()
    same_core(lambda k: f_copy(k).wait_send())
    for k in range(n):
        keep(k).wait()


def finish(
    n, step_ref, loss_ref, grad_ref, queue_ref, arrived_ref, loss_out, grad_out, updated_ref,
    loss_v, loss_w, grad_v, slab, in_sem, out_sem, small_in, small_out,
):
    here = lax.rem(step_ref[0], n) == lax.axis_index("gx")
    pieces = in_sem.shape[0]
    size = slab.shape[0] // pieces

    def part(c):
        return pl.ds(c * size, size)

    def load(src, c):
        return pltpu.make_async_copy(src.at[part(c)], slab.at[part(c)], in_sem.at[c])

    def store(c):
        return pltpu.make_async_copy(slab.at[part(c)], updated_ref.at[part(c)], out_sem.at[c])

    @pl.when(here)
    def _():
        for c in range(pieces):
            load(arrived_ref, c).start()

    @pl.when(jnp.logical_not(here))
    def _():
        for c in range(pieces):
            load(queue_ref, c).start()

    loss_load = pltpu.make_async_copy(loss_ref, loss_v, small_in.at[0])
    grad_load = pltpu.make_async_copy(grad_ref, grad_v, small_in.at[1])
    loss_store = pltpu.make_async_copy(loss_w, loss_out, small_out.at[0])
    grad_store = pltpu.make_async_copy(grad_v, grad_out, small_out.at[1])
    loss_load.start()
    grad_load.start()
    for c in range(pieces):
        load(queue_ref, c).wait()
        store(c).start()
    loss_load.wait()
    loss_w[...] = loss_v[0, 0 : loss_w.shape[0]]
    loss_store.start()
    grad_load.wait()
    grad_store.start()
    for c in range(pieces):
        store(c).wait()
    loss_store.wait()
    grad_store.wait()


def local(n, ngy, queries, positions, queue, new_keys, step):
    q_dev, width = queries.shape
    key_dev = queue.shape[0]
    nk_dev = new_keys.shape[0]
    scale = 2.0 / math.sqrt(width)
    anywhere = pl.BlockSpec(memory_space=pl.ANY)
    vmem = pl.BlockSpec(memory_space=pltpu.VMEM)
    dma = pltpu.SemaphoreType.DMA
    rows = n * q_dev
    loss_row, grad, arrived = pl.pallas_call(
        functools.partial(exchange, n, ngy, scale),
        out_shape=(
            jax.ShapeDtypeStruct((1, LANES), F32),
            jax.ShapeDtypeStruct((q_dev, width), BF16),
            jax.ShapeDtypeStruct((n * ngy, nk_dev, width), BF16),
        ),
        in_specs=[anywhere] * 4,
        out_specs=(vmem, vmem, anywhere),
        scratch_shapes=[
            pltpu.VMEM((n * ngy, nk_dev, width), BF16),
            dma((n,)),
            pltpu.VMEM((key_dev, width), BF16),
            pltpu.VMEM((n, q_dev, width), BF16),
            pltpu.VMEM((n, 1, LANES), jnp.int32),
            pltpu.VMEM((q_dev,), jnp.int32),
            pltpu.VMEM((n, 2, q_dev, width), BF16),
            pltpu.VMEM((n, 2, q_dev, width), BF16),
            pltpu.VMEM((n, 4, LANES), F32),
            pltpu.VMEM((n, 4, LANES), F32),
            dma((4,)),
            dma((n,)), dma((n,)), dma((n,)), dma((n,)),
            dma((ngy,)), dma((ngy,)),
            dma((max(n, 2 * ngy),)), dma((n * ngy,)), dma((ngy,)), dma((n,)), dma((n,)),
            dma((n,)), dma((n,)), dma((n,)), dma((n,)),
        ],
        compiler_params=pltpu.CompilerParams(
            collective_id=0, has_side_effects=True, vmem_limit_bytes=62 * 2**20
        ),
        cost_estimate=pl.CostEstimate(
            flops=6 * rows * key_dev * width,
            bytes_accessed=2 * key_dev * width * 2,
            transcendentals=rows * key_dev,
        ),
        name="exchange",
    )(queries, positions, queue, new_keys)
    return pl.pallas_call(
        functools.partial(finish, n),
        out_shape=(
            jax.ShapeDtypeStruct((q_dev,), F32),
            jax.ShapeDtypeStruct((q_dev, width), BF16),
            jax.ShapeDtypeStruct((key_dev, width), BF16),
        ),
        in_specs=[pl.BlockSpec(memory_space=pltpu.SMEM)] + [anywhere] * 4,
        out_specs=(anywhere,) * 3,
        scratch_shapes=[
            pltpu.VMEM((1, LANES), F32),
            pltpu.VMEM((q_dev,), F32),
            pltpu.VMEM((q_dev, width), BF16),
            pltpu.VMEM((key_dev, width), BF16),
            dma((8,)),
            dma((8,)),
            dma((2,)),
            dma((2,)),
        ],
        compiler_params=pltpu.CompilerParams(vmem_limit_bytes=62 * 2**20),
        name="finish",
    )(step, loss_row, grad, queue, arrived.reshape(key_dev, width))


def solution(mesh):
    return jax.shard_map(
        functools.partial(local, mesh.shape["gx"], mesh.shape["gy"]),
        mesh=mesh,
        in_specs=(
            P(("gx", "gy"), None),
            P(("gx", "gy")),
            P("gx", None),
            P(("gx", "gy"), None),
            P(),
        ),
        out_specs=(P(("gx", "gy")), P(("gx", "gy"), None), P("gx", None)),
        check_vma=False,
    )
```

```python
import functools
import math

import jax
import jax.numpy as jnp
from jax import lax
from jax.experimental import pallas as pl
from jax.experimental.pallas import tpu as pltpu
from jax.sharding import PartitionSpec as P

MESH = pl.DeviceIdType.MESH
LANES = 128
F32 = jnp.float32
BF16 = jnp.bfloat16


def diagonal(rows):
    shape = (rows, LANES)
    return lax.broadcasted_iota(jnp.int32, shape, 0) == lax.broadcasted_iota(jnp.int32, shape, 1)


def to_column(row, diag):
    return jnp.sum(jnp.where(diag, row, 0.0), axis=1, keepdims=True)


def to_row(column, diag):
    return jnp.sum(jnp.where(diag, column, 0.0), axis=0, keepdims=True)


def exchange(
    n, ngy, scale,
    q_ref, pos_ref, queue_ref, nk_ref,
    loss_ref, grad_ref, gathered_ref,
    arrived_ref, keep_sem, keys_t, keys, q_all, p_all, pos_v, part_send, part_recv, stat_send, stat_recv,
    local_sem, q_ss, q_rs, p_ss, p_rs, z_ss, z_rs, k_ss, k_rs, r_ss, f_ss, f_rs, g_ss, g_rs, s_ss, s_rs,
):
    i = lax.axis_index("gx")
    j = lax.axis_index("gy")
    q_dev, width = q_ref.shape
    key_dev = queue_ref.shape[0]

    def send(src, dst, ss, rs, to):
        return pltpu.make_async_remote_copy(
            src_ref=src, dst_ref=dst, send_sem=ss, recv_sem=rs, device_id=to, device_id_type=MESH
        )

    def gx_peers(body):
        for d in range(1, n):
            body(lax.rem(i + d, n))

    def gy_peers(body):
        for d in range(1, ngy):
            body(lax.rem(j + d, ngy))

    load_pos = pltpu.make_async_copy(pos_ref, pos_v, local_sem.at[0])
    load_q = pltpu.make_async_copy(q_ref, q_all.at[i], local_sem.at[1])
    load_keys = pltpu.make_async_copy(queue_ref, keys, local_sem.at[2])
    own_new = pltpu.make_async_copy(nk_ref, arrived_ref.at[i * ngy + j], local_sem.at[3])
    load_pos.start()
    load_q.start()
    load_keys.start()
    own_new.start()

    barrier = pltpu.get_barrier_semaphore()
    gx_peers(lambda p: pl.semaphore_signal(barrier, inc=1, device_id=(p, j), device_id_type=MESH))
    gy_peers(lambda p: pl.semaphore_signal(barrier, inc=1, device_id=(i, p), device_id_type=MESH))
    load_pos.wait()
    load_q.wait()
    diag = diagonal(q_dev)
    p_all[i] = jnp.zeros((1, LANES), jnp.int32)
    p_all[i, :, 0:q_dev] = pos_v[...].reshape(1, q_dev)
    pl.semaphore_wait(barrier, n + ngy - 2)

    def q_copy(p):
        return send(q_all.at[i], q_all.at[i], q_ss.at[p], q_rs.at[i], (p, j))

    def p_copy(p):
        return send(p_all.at[i], p_all.at[i], p_ss.at[p], p_rs.at[i], (p, j))

    def start_queries(p):
        p_copy(p).start()
        q_copy(p).start()

    gx_peers(start_queries)

    square = n == 8
    core = lax.rem(i, 2)
    chip = i // 2
    partner = i + 1 - 2 * core
    low_bit, high_bit = lax.rem(chip, 2), chip // 2
    side_a = (high_bit * 2 + 1 - low_bit) * 2 + core
    side_b = ((1 - high_bit) * 2 + low_bit) * 2 + core

    def wait_in(dst, sem):
        pltpu.make_async_copy(dst, dst, sem).wait()

    def block(k, z):
        return arrived_ref.at[k * ngy + z]

    def rows_of(k):
        return arrived_ref.at[pl.ds(k * ngy, ngy)]

    def z_copy(p):
        return send(block(i, j), block(i, j), z_ss.at[p], z_rs.at[j], (i, p))

    def side_copy(z, side, to):
        return send(block(i, z), block(i, z), k_ss.at[side * ngy + z], k_rs.at[i * ngy + z], (to, j))

    def relay_copy(z):
        k, to = (side_a, side_b) if z % 2 == 0 else (side_b, side_a)
        return send(block(k, z), block(k, z), r_ss.at[z], k_rs.at[k * ngy + z], (to, j))

    def k_copy(p):
        return send(rows_of(i), rows_of(i), k_ss.at[p], k_rs.at[i], (p, j))

    def kept(k):
        return gathered_ref.at[pl.ds(k * ngy, ngy)]

    def f_copy(k):
        return send(rows_of(k), kept(k), f_ss.at[k], f_rs.at[k], (partner, j))

    def keep(k):
        return pltpu.make_async_copy(rows_of(k), kept(k), keep_sem.at[k])

    def same_core(body):
        for d in range(2, n, 2):
            body(lax.rem(i + d, n))

    def to_sides(z):
        side_copy(z, 0, side_a).start()
        side_copy(z, 1, side_b).start()

    own_new.wait()
    gy_peers(lambda p: z_copy(p).start())
    if square:
        to_sides(j)

    def wait_queries(p):
        wait_in(p_all.at[p], p_rs.at[p])
        wait_in(q_all.at[p], q_rs.at[p])

    def spread():
        gy_peers(next_block)
        if not square:
            same_core(lambda p: k_copy(p).start())
        f_copy(i).start()
        keep(i).start()

    def next_block(z):
        wait_in(block(i, z), z_rs.at[z])
        if square:
            to_sides(z)

    load_keys.wait()
    keys_t[...] = keys[...].T

    group = n // 2 if square else min(n, 256 // q_dev)
    rows = group * q_dev

    def work(at):
        columns = [to_column(p_all[at + b].astype(F32), diag) for b in range(group)]
        target = jnp.concatenate(columns, axis=0).astype(jnp.int32) - i * key_dev
        q = q_all[pl.ds(at, group)].reshape(rows, width)
        slab = keys[...]
        scores = jnp.dot(q, keys_t[...], preferred_element_type=F32) * scale
        hits = lax.broadcasted_iota(jnp.int32, scores.shape, 1) == target
        top = jnp.max(scores, axis=1, keepdims=True)
        powers = jnp.exp(scores - top)
        total = jnp.sum(powers, axis=1, keepdims=True)
        others = jnp.where(hits, 0.0, powers).astype(BF16)
        part = jnp.dot(others, slab, preferred_element_type=F32)
        row = jnp.dot(hits.astype(F32).astype(BF16), slab, preferred_element_type=F32)
        positive = jnp.sum(q.astype(F32) * row, axis=1, keepdims=True) * scale
        high = part.astype(BF16)
        low = part - high.astype(F32)
        inside = jnp.logical_and(target >= 0, target < key_dev)
        second = jnp.where(inside, row, low).astype(BF16)
        part_send[pl.ds(at, group), 0] = high.reshape(group, q_dev, width)
        part_send[pl.ds(at, group), 1] = second.reshape(group, q_dev, width)
        for b in range(group):
            span = slice(b * q_dev, (b + 1) * q_dev)
            stat_send[at + b, 0:1] = to_row(top[span], diag)
            stat_send[at + b, 1:2] = to_row(total[span], diag)
            stat_send[at + b, 2:3] = to_row(positive[span], diag)
            stat_send[at + b, 3:4] = jnp.zeros((1, LANES), F32)

    def g_copy(p):
        return send(part_send.at[p], part_recv.at[i], g_ss.at[p], g_rs.at[i], (p, j))

    def s_copy(p):
        return send(stat_send.at[p], stat_recv.at[i], s_ss.at[p], s_rs.at[i], (p, j))

    def start_parts(p):
        s_copy(p).start()
        g_copy(p).start()

    if square:
        far = (1 - high_bit) * group
        for b in range(group):
            wait_queries(far + b)
        work(far)
        for b in range(group):
            start_parts(far + b)
        spread()
        near = high_bit * group
        others = [near + lax.rem(i - near + d, group) for d in range(1, group)]
        for p in others:
            wait_queries(p)
        work(near)
        for p in others:
            start_parts(p)
        for z in range(ngy):
            k = side_a if z % 2 == 0 else side_b
            wait_in(block(k, z), k_rs.at[k * ngy + z])
            relay_copy(z).start()
    else:
        gx_peers(wait_queries)
        spread()
        pl.loop(0, n // group)(lambda c: work(c * group))
        gx_peers(start_parts)
    part_recv[i] = part_send[i]
    stat_recv[i] = stat_send[i]

    def pass_on(k):
        f_copy(k).start()
        keep(k).start()

    if square:
        across = 6 - 2 * chip + core
        for z in range(ngy):
            k = side_b if z % 2 == 0 else side_a
            wait_in(block(k, z), k_rs.at[k * ngy + z])
        pass_on(side_a)
        pass_on(side_b)
        for z in range(ngy):
            wait_in(block(across, z), k_rs.at[across * ngy + z])
        pass_on(across)
    else:
        def receive(k):
            wait_in(rows_of(k), k_rs.at[k])
            pass_on(k)

        same_core(receive)

    gx_peers(lambda p: wait_in(stat_recv.at[p], s_rs.at[p]))
    top = stat_recv[0, 0:1]
    for s in range(1, n):
        top = jnp.maximum(top, stat_recv[s, 0:1])
    total = jnp.zeros_like(top)
    positive = jnp.zeros_like(top)
    for s in range(n):
        total = total + stat_recv[s, 1:2] * jnp.exp(stat_recv[s, 0:1] - top)
        positive = positive + stat_recv[s, 2:3]
    lse = top + jnp.log(total)
    loss_ref[...] = lse - positive
    own = to_column(p_all[i].astype(F32), diag).astype(jnp.int32)
    at_positive = to_column(jnp.exp(positive - lse) - 1.0, diag)
    factors = [to_column(jnp.exp(stat_recv[s, 0:1] - lse), diag) for s in range(n)]

    gx_peers(lambda p: wait_in(part_recv.at[p], g_rs.at[p]))
    grad = jnp.zeros((q_dev, width), F32)
    for s in range(n):
        first = part_recv[s, 0].astype(F32)
        second = part_recv[s, 1].astype(F32)
        inside = jnp.logical_and(own >= s * key_dev, own < (s + 1) * key_dev)
        grad = grad + factors[s] * first + jnp.where(inside, at_positive, factors[s]) * second
    grad_ref[...] = (grad * scale).astype(BF16)

    for d in range(0, n, 2):
        k = lax.rem(partner + d, n)
        wait_in(kept(k), f_rs.at[k])

    def end_sends(p):
        p_copy(p).wait_send()
        q_copy(p).wait_send()
        s_copy(p).wait_send()
        g_copy(p).wait_send()

    gx_peers(end_sends)
    gy_peers(lambda p: z_copy(p).wait_send())
    if square:
        for z in range(ngy):
            side_copy(z, 0, side_a).wait_send()
            side_copy(z, 1, side_b).wait_send()
            relay_copy(z).wait_send()
    else:
        same_core(lambda p: k_copy(p).wait_send())
    f_copy(i).wait_send()
    same_core(lambda k: f_copy(k).wait_send())
    keep(i).wait()
    same_core(lambda k: keep(k).wait())


def finish(
    n, step_ref, loss_ref, grad_ref, queue_ref, arrived_ref, loss_out, grad_out, updated_ref,
    loss_v, loss_w, grad_v, slab, in_sem, out_sem, small_in, small_out,
):
    here = lax.rem(step_ref[0], n) == lax.axis_index("gx")
    pieces = in_sem.shape[0]
    size = slab.shape[0] // pieces

    def part(c):
        return pl.ds(c * size, size)

    def load(src, c):
        return pltpu.make_async_copy(src.at[part(c)], slab.at[part(c)], in_sem.at[c])

    def store(c):
        return pltpu.make_async_copy(slab.at[part(c)], updated_ref.at[part(c)], out_sem.at[c])

    @pl.when(here)
    def _():
        for c in range(pieces):
            load(arrived_ref, c).start()

    @pl.when(jnp.logical_not(here))
    def _():
        for c in range(pieces):
            load(queue_ref, c).start()

    loss_load = pltpu.make_async_copy(loss_ref, loss_v, small_in.at[0])
    grad_load = pltpu.make_async_copy(grad_ref, grad_v, small_in.at[1])
    loss_store = pltpu.make_async_copy(loss_w, loss_out, small_out.at[0])
    grad_store = pltpu.make_async_copy(grad_v, grad_out, small_out.at[1])
    loss_load.start()
    grad_load.start()
    for c in range(pieces):
        load(queue_ref, c).wait()
        store(c).start()
    loss_load.wait()
    loss_w[...] = loss_v[0, 0 : loss_w.shape[0]]
    loss_store.start()
    grad_load.wait()
    grad_store.start()
    for c in range(pieces):
        store(c).wait()
    loss_store.wait()
    grad_store.wait()


def local(n, ngy, queries, positions, queue, new_keys, step):
    q_dev, width = queries.shape
    key_dev = queue.shape[0]
    nk_dev = new_keys.shape[0]
    scale = 2.0 / math.sqrt(width)
    anywhere = pl.BlockSpec(memory_space=pl.ANY)
    vmem = pl.BlockSpec(memory_space=pltpu.VMEM)
    dma = pltpu.SemaphoreType.DMA
    rows = n * q_dev
    loss_row, grad, arrived = pl.pallas_call(
        functools.partial(exchange, n, ngy, scale),
        out_shape=(
            jax.ShapeDtypeStruct((1, LANES), F32),
            jax.ShapeDtypeStruct((q_dev, width), BF16),
            jax.ShapeDtypeStruct((n * ngy, nk_dev, width), BF16),
        ),
        in_specs=[anywhere] * 4,
        out_specs=(vmem, vmem, anywhere),
        scratch_shapes=[
            pltpu.VMEM((n * ngy, nk_dev, width), BF16),
            dma((n,)),
            pltpu.VMEM((width, key_dev), BF16),
            pltpu.VMEM((key_dev, width), BF16),
            pltpu.VMEM((n, q_dev, width), BF16),
            pltpu.VMEM((n, 1, LANES), jnp.int32),
            pltpu.VMEM((q_dev,), jnp.int32),
            pltpu.VMEM((n, 2, q_dev, width), BF16),
            pltpu.VMEM((n, 2, q_dev, width), BF16),
            pltpu.VMEM((n, 4, LANES), F32),
            pltpu.VMEM((n, 4, LANES), F32),
            dma((4,)),
            dma((n,)), dma((n,)), dma((n,)), dma((n,)),
            dma((ngy,)), dma((ngy,)),
            dma((max(n, 2 * ngy),)), dma((n * ngy,)), dma((ngy,)), dma((n,)), dma((n,)),
            dma((n,)), dma((n,)), dma((n,)), dma((n,)),
        ],
        compiler_params=pltpu.CompilerParams(
            collective_id=0, has_side_effects=True, vmem_limit_bytes=62 * 2**20
        ),
        cost_estimate=pl.CostEstimate(
            flops=6 * rows * key_dev * width,
            bytes_accessed=2 * key_dev * width * 2,
            transcendentals=rows * key_dev,
        ),
        name="exchange",
    )(queries, positions, queue, new_keys)
    return pl.pallas_call(
        functools.partial(finish, n),
        out_shape=(
            jax.ShapeDtypeStruct((q_dev,), F32),
            jax.ShapeDtypeStruct((q_dev, width), BF16),
            jax.ShapeDtypeStruct((key_dev, width), BF16),
        ),
        in_specs=[pl.BlockSpec(memory_space=pltpu.SMEM)] + [anywhere] * 4,
        out_specs=(anywhere,) * 3,
        scratch_shapes=[
            pltpu.VMEM((1, LANES), F32),
            pltpu.VMEM((q_dev,), F32),
            pltpu.VMEM((q_dev, width), BF16),
            pltpu.VMEM((key_dev, width), BF16),
            dma((8,)),
            dma((8,)),
            dma((2,)),
            dma((2,)),
        ],
        compiler_params=pltpu.CompilerParams(vmem_limit_bytes=62 * 2**20),
        name="finish",
    )(step, loss_row, grad, queue, arrived.reshape(key_dev, width))


def solution(mesh):
    return jax.shard_map(
        functools.partial(local, mesh.shape["gx"], mesh.shape["gy"]),
        mesh=mesh,
        in_specs=(
            P(("gx", "gy"), None),
            P(("gx", "gy")),
            P("gx", None),
            P(("gx", "gy"), None),
            P(),
        ),
        out_specs=(P(("gx", "gy")), P(("gx", "gy"), None), P("gx", None)),
        check_vma=False,
    )
```

```python
import functools
import math

import jax
import jax.numpy as jnp
from jax import lax
from jax.experimental import pallas as pl
from jax.experimental.pallas import tpu as pltpu
from jax.sharding import PartitionSpec as P

MESH = pl.DeviceIdType.MESH
LANES = 128
F32 = jnp.float32
BF16 = jnp.bfloat16


def diagonal(rows):
    shape = (rows, LANES)
    return lax.broadcasted_iota(jnp.int32, shape, 0) == lax.broadcasted_iota(jnp.int32, shape, 1)


def to_column(row, diag):
    return jnp.sum(jnp.where(diag, row, 0.0), axis=1, keepdims=True)


def to_row(column, diag):
    return jnp.sum(jnp.where(diag, column, 0.0), axis=0, keepdims=True)


def exchange(
    n, ngy, scale,
    q_ref, pos_ref, queue_ref, nk_ref,
    loss_ref, grad_ref, gathered_ref,
    arrived_ref, keep_sem, keys, q_all, p_all, pos_v, part_send, part_recv, stat_send, stat_recv,
    local_sem, q_ss, q_rs, p_ss, p_rs, z_ss, z_rs, k_ss, k_rs, f_ss, f_rs, g_ss, g_rs, s_ss, s_rs,
):
    i = lax.axis_index("gx")
    j = lax.axis_index("gy")
    q_dev, width = q_ref.shape
    key_dev = queue_ref.shape[0]

    def send(src, dst, ss, rs, to):
        return pltpu.make_async_remote_copy(
            src_ref=src, dst_ref=dst, send_sem=ss, recv_sem=rs, device_id=to, device_id_type=MESH
        )

    def gx_peers(body):
        for d in range(1, n):
            body(lax.rem(i + d, n))

    def gy_peers(body):
        for d in range(1, ngy):
            body(lax.rem(j + d, ngy))

    load_pos = pltpu.make_async_copy(pos_ref, pos_v, local_sem.at[0])
    load_q = pltpu.make_async_copy(q_ref, q_all.at[i], local_sem.at[1])
    load_keys = pltpu.make_async_copy(queue_ref, keys, local_sem.at[2])
    own_new = pltpu.make_async_copy(nk_ref, arrived_ref.at[i * ngy + j], local_sem.at[3])
    load_pos.start()
    load_q.start()
    load_keys.start()
    own_new.start()

    barrier = pltpu.get_barrier_semaphore()
    gx_peers(lambda p: pl.semaphore_signal(barrier, inc=1, device_id=(p, j), device_id_type=MESH))
    gy_peers(lambda p: pl.semaphore_signal(barrier, inc=1, device_id=(i, p), device_id_type=MESH))
    load_pos.wait()
    load_q.wait()
    diag = diagonal(q_dev)
    p_all[i] = jnp.zeros((1, LANES), jnp.int32)
    p_all[i, :, 0:q_dev] = pos_v[...].reshape(1, q_dev)
    pl.semaphore_wait(barrier, n + ngy - 2)

    def q_copy(p):
        return send(q_all.at[i], q_all.at[i], q_ss.at[p], q_rs.at[i], (p, j))

    def p_copy(p):
        return send(p_all.at[i], p_all.at[i], p_ss.at[p], p_rs.at[i], (p, j))

    def start_queries(p):
        p_copy(p).start()
        q_copy(p).start()

    gx_peers(start_queries)

    by_block = n * ngy <= 32
    core = lax.rem(i, 2)
    partner = i + 1 - 2 * core

    def wait_in(dst, sem):
        pltpu.make_async_copy(dst, dst, sem).wait()

    def block(k, z):
        return arrived_ref.at[k * ngy + z]

    def rows_of(k):
        return arrived_ref.at[pl.ds(k * ngy, ngy)]

    def z_copy(p):
        return send(block(i, j), block(i, j), z_ss.at[p], z_rs.at[j], (i, p))

    def b_copy(p, z):
        return send(block(i, z), block(i, z), k_ss.at[p * ngy + z], k_rs.at[i * ngy + z], (p, j))

    def k_copy(p):
        return send(rows_of(i), rows_of(i), k_ss.at[p], k_rs.at[i], (p, j))

    def kept(k):
        return gathered_ref.at[pl.ds(k * ngy, ngy)]

    def f_copy(k):
        return send(rows_of(k), kept(k), f_ss.at[k], f_rs.at[k], (partner, j))

    def keep(k):
        return pltpu.make_async_copy(rows_of(k), kept(k), keep_sem.at[k])

    def same_core(body):
        for d in range(2, n, 2):
            body(lax.rem(i + d, n))

    def go_on(z):
        same_core(lambda p: b_copy(p, z).start())

    own_new.wait()
    gy_peers(lambda p: z_copy(p).start())
    if by_block:
        go_on(j)

    def wait_queries(p):
        wait_in(p_all.at[p], p_rs.at[p])
        wait_in(q_all.at[p], q_rs.at[p])

    def next_block(z):
        wait_in(block(i, z), z_rs.at[z])
        if by_block:
            go_on(z)

    gy_peers(next_block)
    if not by_block:
        same_core(lambda p: k_copy(p).start())
    f_copy(i).start()
    keep(i).start()
    gx_peers(wait_queries)
    load_keys.wait()

    group = min(n, 256 // q_dev)
    rows = group * q_dev

    def work(at):
        columns = [to_column(p_all[at + b].astype(F32), diag) for b in range(group)]
        target = jnp.concatenate(columns, axis=0).astype(jnp.int32) - i * key_dev
        q = q_all[pl.ds(at, group)].reshape(rows, width)
        slab = keys[...]
        scores = lax.dot_general(q, slab, (((1,), (1,)), ((), ())), preferred_element_type=F32) * scale
        hits = lax.broadcasted_iota(jnp.int32, scores.shape, 1) == target
        top = jnp.max(scores, axis=1, keepdims=True)
        powers = jnp.exp(scores - top)
        total = jnp.sum(powers, axis=1, keepdims=True)
        others = jnp.where(hits, 0.0, powers).astype(BF16)
        part = jnp.dot(others, slab, preferred_element_type=F32)
        row = jnp.dot(hits.astype(F32).astype(BF16), slab, preferred_element_type=F32)
        positive = jnp.sum(q.astype(F32) * row, axis=1, keepdims=True) * scale
        high = part.astype(BF16)
        low = part - high.astype(F32)
        inside = jnp.logical_and(target >= 0, target < key_dev)
        second = jnp.where(inside, row, low).astype(BF16)
        part_send[pl.ds(at, group), 0] = high.reshape(group, q_dev, width)
        part_send[pl.ds(at, group), 1] = second.reshape(group, q_dev, width)
        for b in range(group):
            span = slice(b * q_dev, (b + 1) * q_dev)
            stat_send[at + b, 0:1] = to_row(top[span], diag)
            stat_send[at + b, 1:2] = to_row(total[span], diag)
            stat_send[at + b, 2:3] = to_row(positive[span], diag)
            stat_send[at + b, 3:4] = jnp.zeros((1, LANES), F32)

    def g_copy(p):
        return send(part_send.at[p], part_recv.at[i], g_ss.at[p], g_rs.at[i], (p, j))

    def s_copy(p):
        return send(stat_send.at[p], stat_recv.at[i], s_ss.at[p], s_rs.at[i], (p, j))

    def start_parts(p):
        s_copy(p).start()
        g_copy(p).start()

    if n == group:
        work(0)
    else:
        pl.loop(0, n // group)(lambda c: work(c * group))
    gx_peers(start_parts)
    part_recv[i] = part_send[i]
    stat_recv[i] = stat_send[i]

    def pass_on(k):
        if by_block:
            for z in range(ngy):
                wait_in(block(k, z), k_rs.at[k * ngy + z])
        else:
            wait_in(rows_of(k), k_rs.at[k])
        f_copy(k).start()
        keep(k).start()

    same_core(pass_on)

    gx_peers(lambda p: wait_in(stat_recv.at[p], s_rs.at[p]))
    top = stat_recv[0, 0:1]
    for s in range(1, n):
        top = jnp.maximum(top, stat_recv[s, 0:1])
    total = jnp.zeros_like(top)
    positive = jnp.zeros_like(top)
    for s in range(n):
        total = total + stat_recv[s, 1:2] * jnp.exp(stat_recv[s, 0:1] - top)
        positive = positive + stat_recv[s, 2:3]
    lse = top + jnp.log(total)
    loss_ref[...] = lse - positive
    own = to_column(p_all[i].astype(F32), diag).astype(jnp.int32)
    at_positive = to_column(jnp.exp(positive - lse) - 1.0, diag)
    factors = [to_column(jnp.exp(stat_recv[s, 0:1] - lse), diag) for s in range(n)]

    gx_peers(lambda p: wait_in(part_recv.at[p], g_rs.at[p]))
    grad = jnp.zeros((q_dev, width), F32)
    for s in range(n):
        first = part_recv[s, 0].astype(F32)
        second = part_recv[s, 1].astype(F32)
        inside = jnp.logical_and(own >= s * key_dev, own < (s + 1) * key_dev)
        grad = grad + factors[s] * first + jnp.where(inside, at_positive, factors[s]) * second
    grad_ref[...] = (grad * scale).astype(BF16)

    for d in range(0, n, 2):
        k = lax.rem(partner + d, n)
        wait_in(kept(k), f_rs.at[k])

    def end_sends(p):
        p_copy(p).wait_send()
        q_copy(p).wait_send()
        s_copy(p).wait_send()
        g_copy(p).wait_send()

    gx_peers(end_sends)
    gy_peers(lambda p: z_copy(p).wait_send())
    if by_block:
        for z in range(ngy):
            same_core(lambda p: b_copy(p, z).wait_send())
    else:
        same_core(lambda p: k_copy(p).wait_send())
    f_copy(i).wait_send()
    same_core(lambda k: f_copy(k).wait_send())
    keep(i).wait()
    same_core(lambda k: keep(k).wait())


def finish(
    n, step_ref, loss_ref, grad_ref, queue_ref, arrived_ref, loss_out, grad_out, updated_ref,
    loss_v, loss_w, grad_v, slab, in_sem, out_sem, small_in, small_out,
):
    here = lax.rem(step_ref[0], n) == lax.axis_index("gx")
    pieces = in_sem.shape[0]
    size = slab.shape[0] // pieces

    def part(c):
        return pl.ds(c * size, size)

    def load(src, c):
        return pltpu.make_async_copy(src.at[part(c)], slab.at[part(c)], in_sem.at[c])

    def store(c):
        return pltpu.make_async_copy(slab.at[part(c)], updated_ref.at[part(c)], out_sem.at[c])

    @pl.when(here)
    def _():
        for c in range(pieces):
            load(arrived_ref, c).start()

    @pl.when(jnp.logical_not(here))
    def _():
        for c in range(pieces):
            load(queue_ref, c).start()

    loss_load = pltpu.make_async_copy(loss_ref, loss_v, small_in.at[0])
    grad_load = pltpu.make_async_copy(grad_ref, grad_v, small_in.at[1])
    loss_store = pltpu.make_async_copy(loss_w, loss_out, small_out.at[0])
    grad_store = pltpu.make_async_copy(grad_v, grad_out, small_out.at[1])
    loss_load.start()
    grad_load.start()
    for c in range(pieces):
        load(queue_ref, c).wait()
        store(c).start()
    loss_load.wait()
    loss_w[...] = loss_v[0, 0 : loss_w.shape[0]]
    loss_store.start()
    grad_load.wait()
    grad_store.start()
    for c in range(pieces):
        store(c).wait()
    loss_store.wait()
    grad_store.wait()


def local(n, ngy, queries, positions, queue, new_keys, step):
    q_dev, width = queries.shape
    key_dev = queue.shape[0]
    nk_dev = new_keys.shape[0]
    scale = 2.0 / math.sqrt(width)
    anywhere = pl.BlockSpec(memory_space=pl.ANY)
    vmem = pl.BlockSpec(memory_space=pltpu.VMEM)
    dma = pltpu.SemaphoreType.DMA
    rows = n * q_dev
    loss_row, grad, arrived = pl.pallas_call(
        functools.partial(exchange, n, ngy, scale),
        out_shape=(
            jax.ShapeDtypeStruct((1, LANES), F32),
            jax.ShapeDtypeStruct((q_dev, width), BF16),
            jax.ShapeDtypeStruct((n * ngy, nk_dev, width), BF16),
        ),
        in_specs=[anywhere] * 4,
        out_specs=(vmem, vmem, anywhere),
        scratch_shapes=[
            pltpu.VMEM((n * ngy, nk_dev, width), BF16),
            dma((n,)),
            pltpu.VMEM((key_dev, width), BF16),
            pltpu.VMEM((n, q_dev, width), BF16),
            pltpu.VMEM((n, 1, LANES), jnp.int32),
            pltpu.VMEM((q_dev,), jnp.int32),
            pltpu.VMEM((n, 2, q_dev, width), BF16),
            pltpu.VMEM((n, 2, q_dev, width), BF16),
            pltpu.VMEM((n, 4, LANES), F32),
            pltpu.VMEM((n, 4, LANES), F32),
            dma((4,)),
            dma((n,)), dma((n,)), dma((n,)), dma((n,)),
            dma((ngy,)), dma((ngy,)),
            dma((n * ngy,)), dma((n * ngy,)), dma((n,)), dma((n,)),
            dma((n,)), dma((n,)), dma((n,)), dma((n,)),
        ],
        compiler_params=pltpu.CompilerParams(
            collective_id=0, has_side_effects=True, vmem_limit_bytes=62 * 2**20
        ),
        cost_estimate=pl.CostEstimate(
            flops=6 * rows * key_dev * width,
            bytes_accessed=2 * key_dev * width * 2,
            transcendentals=rows * key_dev,
        ),
        name="exchange",
    )(queries, positions, queue, new_keys)
    return pl.pallas_call(
        functools.partial(finish, n),
        out_shape=(
            jax.ShapeDtypeStruct((q_dev,), F32),
            jax.ShapeDtypeStruct((q_dev, width), BF16),
            jax.ShapeDtypeStruct((key_dev, width), BF16),
        ),
        in_specs=[pl.BlockSpec(memory_space=pltpu.SMEM)] + [anywhere] * 4,
        out_specs=(anywhere,) * 3,
        scratch_shapes=[
            pltpu.VMEM((1, LANES), F32),
            pltpu.VMEM((q_dev,), F32),
            pltpu.VMEM((q_dev, width), BF16),
            pltpu.VMEM((key_dev, width), BF16),
            dma((8,)),
            dma((8,)),
            dma((2,)),
            dma((2,)),
        ],
        compiler_params=pltpu.CompilerParams(vmem_limit_bytes=62 * 2**20),
        name="finish",
    )(step, loss_row, grad, queue, arrived.reshape(key_dev, width))


def solution(mesh):
    return jax.shard_map(
        functools.partial(local, mesh.shape["gx"], mesh.shape["gy"]),
        mesh=mesh,
        in_specs=(
            P(("gx", "gy"), None),
            P(("gx", "gy")),
            P("gx", None),
            P(("gx", "gy"), None),
            P(),
        ),
        out_specs=(P(("gx", "gy")), P(("gx", "gy"), None), P("gx", None)),
        check_vma=False,
    )
```

```python
import functools
import math

import jax
import jax.numpy as jnp
from jax import lax
from jax.experimental import pallas as pl
from jax.experimental.pallas import tpu as pltpu
from jax.sharding import PartitionSpec as P

MESH = pl.DeviceIdType.MESH
LANES = 128
F32 = jnp.float32
BF16 = jnp.bfloat16


def diagonal(rows):
    shape = (rows, LANES)
    return lax.broadcasted_iota(jnp.int32, shape, 0) == lax.broadcasted_iota(jnp.int32, shape, 1)


def to_column(row, diag):
    return jnp.sum(jnp.where(diag, row, 0.0), axis=1, keepdims=True)


def to_row(column, diag):
    return jnp.sum(jnp.where(diag, column, 0.0), axis=0, keepdims=True)


def exchange(
    n, ngy, scale,
    q_ref, pos_ref, queue_ref, nk_ref,
    loss_ref, grad_ref, gathered_ref,
    arrived_ref, keep_sem, keys, q_all, p_all, pos_v, part_send, part_recv, stat_send, stat_recv,
    local_sem, q_ss, q_rs, p_ss, p_rs, z_ss, z_rs, k_ss, k_rs, f_ss, f_rs, g_ss, g_rs, s_ss, s_rs,
):
    i = lax.axis_index("gx")
    j = lax.axis_index("gy")
    q_dev, width = q_ref.shape
    key_dev = queue_ref.shape[0]

    def send(src, dst, ss, rs, to):
        return pltpu.make_async_remote_copy(
            src_ref=src, dst_ref=dst, send_sem=ss, recv_sem=rs, device_id=to, device_id_type=MESH
        )

    def gx_peers(body):
        for d in range(1, n):
            body(lax.rem(i + d, n))

    def gy_peers(body):
        for d in range(1, ngy):
            body(lax.rem(j + d, ngy))

    load_pos = pltpu.make_async_copy(pos_ref, pos_v, local_sem.at[0])
    load_q = pltpu.make_async_copy(q_ref, q_all.at[i], local_sem.at[1])
    load_keys = pltpu.make_async_copy(queue_ref, keys, local_sem.at[2])
    own_new = pltpu.make_async_copy(nk_ref, arrived_ref.at[i * ngy + j], local_sem.at[3])
    load_pos.start()
    load_q.start()
    load_keys.start()
    own_new.start()

    barrier = pltpu.get_barrier_semaphore()
    gx_peers(lambda p: pl.semaphore_signal(barrier, inc=1, device_id=(p, j), device_id_type=MESH))
    gy_peers(lambda p: pl.semaphore_signal(barrier, inc=1, device_id=(i, p), device_id_type=MESH))
    load_pos.wait()
    load_q.wait()
    diag = diagonal(q_dev)
    p_all[i] = jnp.zeros((1, LANES), jnp.int32)
    p_all[i, :, 0:q_dev] = pos_v[...].reshape(1, q_dev)
    pl.semaphore_wait(barrier, n + ngy - 2)

    def q_copy(p):
        return send(q_all.at[i], q_all.at[i], q_ss.at[p], q_rs.at[i], (p, j))

    def p_copy(p):
        return send(p_all.at[i], p_all.at[i], p_ss.at[p], p_rs.at[i], (p, j))

    by_block = n * ngy <= 32
    core = lax.rem(i, 2)
    partner = i + 1 - 2 * core

    def wait_in(dst, sem):
        pltpu.make_async_copy(dst, dst, sem).wait()

    def block(k, z):
        return arrived_ref.at[k * ngy + z]

    def rows_of(k):
        return arrived_ref.at[pl.ds(k * ngy, ngy)]

    def z_copy(p):
        return send(block(i, j), block(i, j), z_ss.at[p], z_rs.at[j], (i, p))

    def b_copy(p, z):
        return send(block(i, z), block(i, z), k_ss.at[p * ngy + z], k_rs.at[i * ngy + z], (p, j))

    def k_copy(p):
        return send(rows_of(i), rows_of(i), k_ss.at[p], k_rs.at[i], (p, j))

    def kept(k):
        return gathered_ref.at[pl.ds(k * ngy, ngy)]

    def f_copy(k):
        return send(rows_of(k), kept(k), f_ss.at[k], f_rs.at[k], (partner, j))

    def keep(k):
        return pltpu.make_async_copy(rows_of(k), kept(k), keep_sem.at[k])

    def same_core(body):
        for d in range(2, n, 2):
            body(lax.rem(i + d, n))

    def go_on(z):
        same_core(lambda p: b_copy(p, z).start())

    group = min(n, 256 // q_dev)
    rows = group * q_dev

    def find(at):
        columns = [to_column(p_all[at + b].astype(F32), diag) for b in range(group)]
        target = jnp.concatenate(columns, axis=0).astype(jnp.int32) - i * key_dev
        hits = lax.broadcasted_iota(jnp.int32, (rows, key_dev), 1) == target
        row = jnp.dot(hits.astype(F32).astype(BF16), keys[...], preferred_element_type=F32)
        return target, row

    def work(at, found, start_stats):
        target, row = found
        q = q_all[pl.ds(at, group)].reshape(rows, width)
        slab = keys[...]
        raw = lax.dot_general(q, slab, (((1,), (1,)), ((), ())), preferred_element_type=F32)
        hits = lax.broadcasted_iota(jnp.int32, raw.shape, 1) == target
        top = jnp.max(raw, axis=1, keepdims=True)
        powers = jnp.exp2((raw - top) * (scale * math.log2(math.e)))
        total = jnp.sum(powers, axis=1, keepdims=True)
        others = jnp.where(hits, 0.0, powers).astype(BF16)
        positive = jnp.sum(jnp.where(hits, raw, 0.0), axis=1, keepdims=True)
        for b in range(group):
            span = slice(b * q_dev, (b + 1) * q_dev)
            stat_send[at + b, 0:1] = to_row(top[span], diag) * scale
            stat_send[at + b, 1:2] = to_row(total[span], diag)
            stat_send[at + b, 2:3] = to_row(positive[span], diag) * scale
            stat_send[at + b, 3:4] = jnp.zeros((1, LANES), F32)
        start_stats()
        part = jnp.dot(others, slab, preferred_element_type=F32)
        high = part.astype(BF16)
        low = part - high.astype(F32)
        inside = jnp.logical_and(target >= 0, target < key_dev)
        second = jnp.where(inside, row, low).astype(BF16)
        part_send[pl.ds(at, group), 0] = high.reshape(group, q_dev, width)
        part_send[pl.ds(at, group), 1] = second.reshape(group, q_dev, width)

    def g_copy(p):
        return send(part_send.at[p], part_recv.at[i], g_ss.at[p], g_rs.at[i], (p, j))

    def s_copy(p):
        return send(stat_send.at[p], stat_recv.at[i], s_ss.at[p], s_rs.at[i], (p, j))

    def next_block(z):
        wait_in(block(i, z), z_rs.at[z])
        if by_block:
            go_on(z)

    own_new.wait()
    gy_peers(lambda p: z_copy(p).start())
    gx_peers(lambda p: p_copy(p).start())
    gx_peers(lambda p: q_copy(p).start())
    if by_block:
        go_on(j)
    load_keys.wait()
    gx_peers(lambda p: wait_in(p_all.at[p], p_rs.at[p]))
    whole = n == group
    if whole:
        found = find(0)
    gy_peers(next_block)
    if not by_block:
        same_core(lambda p: k_copy(p).start())
    f_copy(i).start()
    keep(i).start()
    gx_peers(lambda p: wait_in(q_all.at[p], q_rs.at[p]))
    if whole:
        work(0, found, lambda: gx_peers(lambda p: s_copy(p).start()))
    else:
        pl.loop(0, n // group)(lambda c: work(c * group, find(c * group), lambda: None))
        gx_peers(lambda p: s_copy(p).start())
    gx_peers(lambda p: g_copy(p).start())
    part_recv[i] = part_send[i]
    stat_recv[i] = stat_send[i]

    def pass_on(k):
        if by_block:
            for z in range(ngy):
                wait_in(block(k, z), k_rs.at[k * ngy + z])
        else:
            wait_in(rows_of(k), k_rs.at[k])
        f_copy(k).start()
        keep(k).start()

    same_core(pass_on)

    gx_peers(lambda p: wait_in(stat_recv.at[p], s_rs.at[p]))
    top = stat_recv[0, 0:1]
    for s in range(1, n):
        top = jnp.maximum(top, stat_recv[s, 0:1])
    total = jnp.zeros_like(top)
    positive = jnp.zeros_like(top)
    for s in range(n):
        total = total + stat_recv[s, 1:2] * jnp.exp(stat_recv[s, 0:1] - top)
        positive = positive + stat_recv[s, 2:3]
    lse = top + jnp.log(total)
    loss_ref[...] = lse - positive
    own = to_column(p_all[i].astype(F32), diag).astype(jnp.int32)
    at_positive = to_column(jnp.exp(positive - lse) - 1.0, diag)
    factors = [to_column(jnp.exp(stat_recv[s, 0:1] - lse), diag) for s in range(n)]

    gx_peers(lambda p: wait_in(part_recv.at[p], g_rs.at[p]))
    grad = jnp.zeros((q_dev, width), F32)
    for s in range(n):
        first = part_recv[s, 0].astype(F32)
        second = part_recv[s, 1].astype(F32)
        inside = jnp.logical_and(own >= s * key_dev, own < (s + 1) * key_dev)
        grad = grad + factors[s] * first + jnp.where(inside, at_positive, factors[s]) * second
    grad_ref[...] = (grad * scale).astype(BF16)

    for d in range(0, n, 2):
        k = lax.rem(partner + d, n)
        wait_in(kept(k), f_rs.at[k])

    def end_sends(p):
        p_copy(p).wait_send()
        q_copy(p).wait_send()
        s_copy(p).wait_send()
        g_copy(p).wait_send()

    gx_peers(end_sends)
    gy_peers(lambda p: z_copy(p).wait_send())
    if by_block:
        for z in range(ngy):
            same_core(lambda p: b_copy(p, z).wait_send())
    else:
        same_core(lambda p: k_copy(p).wait_send())
    f_copy(i).wait_send()
    same_core(lambda k: f_copy(k).wait_send())
    keep(i).wait()
    same_core(lambda k: keep(k).wait())


def finish(
    n, step_ref, loss_ref, grad_ref, queue_ref, arrived_ref, loss_out, grad_out, updated_ref,
    loss_v, loss_w, grad_v, slab, in_sem, out_sem, small_in, small_out,
):
    here = lax.rem(step_ref[0], n) == lax.axis_index("gx")
    pieces = in_sem.shape[0]
    size = slab.shape[0] // pieces

    def part(c):
        return pl.ds(c * size, size)

    def load(src, c):
        return pltpu.make_async_copy(src.at[part(c)], slab.at[part(c)], in_sem.at[c])

    def store(c):
        return pltpu.make_async_copy(slab.at[part(c)], updated_ref.at[part(c)], out_sem.at[c])

    @pl.when(here)
    def _():
        for c in range(pieces):
            load(arrived_ref, c).start()

    @pl.when(jnp.logical_not(here))
    def _():
        for c in range(pieces):
            load(queue_ref, c).start()

    loss_load = pltpu.make_async_copy(loss_ref, loss_v, small_in.at[0])
    grad_load = pltpu.make_async_copy(grad_ref, grad_v, small_in.at[1])
    loss_store = pltpu.make_async_copy(loss_w, loss_out, small_out.at[0])
    grad_store = pltpu.make_async_copy(grad_v, grad_out, small_out.at[1])
    loss_load.start()
    grad_load.start()
    for c in range(pieces):
        load(queue_ref, c).wait()
        store(c).start()
    loss_load.wait()
    loss_w[...] = loss_v[0, 0 : loss_w.shape[0]]
    loss_store.start()
    grad_load.wait()
    grad_store.start()
    for c in range(pieces):
        store(c).wait()
    loss_store.wait()
    grad_store.wait()


def local(n, ngy, queries, positions, queue, new_keys, step):
    q_dev, width = queries.shape
    key_dev = queue.shape[0]
    nk_dev = new_keys.shape[0]
    scale = 2.0 / math.sqrt(width)
    anywhere = pl.BlockSpec(memory_space=pl.ANY)
    vmem = pl.BlockSpec(memory_space=pltpu.VMEM)
    dma = pltpu.SemaphoreType.DMA
    rows = n * q_dev
    loss_row, grad, arrived = pl.pallas_call(
        functools.partial(exchange, n, ngy, scale),
        out_shape=(
            jax.ShapeDtypeStruct((1, LANES), F32),
            jax.ShapeDtypeStruct((q_dev, width), BF16),
            jax.ShapeDtypeStruct((n * ngy, nk_dev, width), BF16),
        ),
        in_specs=[anywhere] * 4,
        out_specs=(vmem, vmem, anywhere),
        scratch_shapes=[
            pltpu.VMEM((n * ngy, nk_dev, width), BF16),
            dma((n,)),
            pltpu.VMEM((key_dev, width), BF16),
            pltpu.VMEM((n, q_dev, width), BF16),
            pltpu.VMEM((n, 1, LANES), jnp.int32),
            pltpu.VMEM((q_dev,), jnp.int32),
            pltpu.VMEM((n, 2, q_dev, width), BF16),
            pltpu.VMEM((n, 2, q_dev, width), BF16),
            pltpu.VMEM((n, 4, LANES), F32),
            pltpu.VMEM((n, 4, LANES), F32),
            dma((4,)),
            dma((n,)), dma((n,)), dma((n,)), dma((n,)),
            dma((ngy,)), dma((ngy,)),
            dma((n * ngy,)), dma((n * ngy,)), dma((n,)), dma((n,)),
            dma((n,)), dma((n,)), dma((n,)), dma((n,)),
        ],
        compiler_params=pltpu.CompilerParams(
            collective_id=0, has_side_effects=True, vmem_limit_bytes=62 * 2**20
        ),
        cost_estimate=pl.CostEstimate(
            flops=6 * rows * key_dev * width,
            bytes_accessed=2 * key_dev * width * 2,
            transcendentals=rows * key_dev,
        ),
        name="exchange",
    )(queries, positions, queue, new_keys)
    return pl.pallas_call(
        functools.partial(finish, n),
        out_shape=(
            jax.ShapeDtypeStruct((q_dev,), F32),
            jax.ShapeDtypeStruct((q_dev, width), BF16),
            jax.ShapeDtypeStruct((key_dev, width), BF16),
        ),
        in_specs=[pl.BlockSpec(memory_space=pltpu.SMEM)] + [anywhere] * 4,
        out_specs=(anywhere,) * 3,
        scratch_shapes=[
            pltpu.VMEM((1, LANES), F32),
            pltpu.VMEM((q_dev,), F32),
            pltpu.VMEM((q_dev, width), BF16),
            pltpu.VMEM((key_dev, width), BF16),
            dma((8,)),
            dma((8,)),
            dma((2,)),
            dma((2,)),
        ],
        compiler_params=pltpu.CompilerParams(vmem_limit_bytes=62 * 2**20),
        name="finish",
    )(step, loss_row, grad, queue, arrived.reshape(key_dev, width))


def solution(mesh):
    return jax.shard_map(
        functools.partial(local, mesh.shape["gx"], mesh.shape["gy"]),
        mesh=mesh,
        in_specs=(
            P(("gx", "gy"), None),
            P(("gx", "gy")),
            P("gx", None),
            P(("gx", "gy"), None),
            P(),
        ),
        out_specs=(P(("gx", "gy")), P(("gx", "gy"), None), P("gx", None)),
        check_vma=False,
    )
```

```python
import functools
import math

import jax
import jax.numpy as jnp
from jax import lax
from jax.experimental import pallas as pl
from jax.experimental.pallas import tpu as pltpu
from jax.sharding import PartitionSpec as P

MESH = pl.DeviceIdType.MESH
LANES = 128
F32 = jnp.float32
BF16 = jnp.bfloat16


def diagonal(rows):
    shape = (rows, LANES)
    return lax.broadcasted_iota(jnp.int32, shape, 0) == lax.broadcasted_iota(jnp.int32, shape, 1)


def to_column(row, diag):
    return jnp.sum(jnp.where(diag, row, 0.0), axis=1, keepdims=True)


def to_row(column, diag):
    return jnp.sum(jnp.where(diag, column, 0.0), axis=0, keepdims=True)


def exchange(
    n, ngy, scale,
    q_ref, pos_ref, queue_ref, nk_ref,
    loss_out, grad_out, gathered_ref,
    loss_ref, grad_ref, result_sem, arrived_ref, keep_sem, keys, q_all, p_all, pos_v, part_send, part_recv, stat_send, stat_recv,
    local_sem, q_ss, q_rs, p_ss, p_rs, z_ss, z_rs, k_ss, k_rs, f_ss, f_rs, g_ss, g_rs, s_ss, s_rs,
):
    i = lax.axis_index("gx")
    j = lax.axis_index("gy")
    q_dev, width = q_ref.shape
    key_dev = queue_ref.shape[0]

    def send(src, dst, ss, rs, to):
        return pltpu.make_async_remote_copy(
            src_ref=src, dst_ref=dst, send_sem=ss, recv_sem=rs, device_id=to, device_id_type=MESH
        )

    def gx_peers(body):
        for d in range(1, n):
            body(lax.rem(i + d, n))

    def gy_peers(body):
        turn = 1 - 2 * ((2 * j) // ngy)
        for d in range(1, ngy):
            body(lax.rem(j + turn * d + ngy, ngy))

    load_pos = pltpu.make_async_copy(pos_ref, pos_v, local_sem.at[0])
    load_q = pltpu.make_async_copy(q_ref, q_all.at[i], local_sem.at[1])
    load_keys = pltpu.make_async_copy(queue_ref, keys, local_sem.at[2])
    own_new = pltpu.make_async_copy(nk_ref, arrived_ref.at[i * ngy + j], local_sem.at[3])
    load_pos.start()
    load_q.start()
    load_keys.start()
    own_new.start()

    barrier = pltpu.get_barrier_semaphore()
    gx_peers(lambda p: pl.semaphore_signal(barrier, inc=1, device_id=(p, j), device_id_type=MESH))
    gy_peers(lambda p: pl.semaphore_signal(barrier, inc=1, device_id=(i, p), device_id_type=MESH))
    load_pos.wait()
    load_q.wait()
    diag = diagonal(q_dev)
    p_all[i] = jnp.zeros((1, LANES), jnp.int32)
    p_all[i, :, 0:q_dev] = pos_v[...].reshape(1, q_dev)
    pl.semaphore_wait(barrier, n + ngy - 2)

    def q_copy(p):
        return send(q_all.at[i], q_all.at[i], q_ss.at[p], q_rs.at[i], (p, j))

    def p_copy(p):
        return send(p_all.at[i], p_all.at[i], p_ss.at[p], p_rs.at[i], (p, j))

    by_block = n * ngy <= 32
    core = lax.rem(i, 2)
    partner = i + 1 - 2 * core

    def wait_in(dst, sem):
        pltpu.make_async_copy(dst, dst, sem).wait()

    def block(k, z):
        return arrived_ref.at[k * ngy + z]

    def rows_of(k):
        return arrived_ref.at[pl.ds(k * ngy, ngy)]

    def z_copy(p):
        return send(block(i, j), block(i, j), z_ss.at[p], z_rs.at[j], (i, p))

    def b_copy(p, z):
        return send(block(i, z), block(i, z), k_ss.at[p * ngy + z], k_rs.at[i * ngy + z], (p, j))

    def k_copy(p):
        return send(rows_of(i), rows_of(i), k_ss.at[p], k_rs.at[i], (p, j))

    def kept(k):
        return gathered_ref.at[pl.ds(k * ngy, ngy)]

    def f_copy(k):
        return send(rows_of(k), kept(k), f_ss.at[k], f_rs.at[k], (partner, j))

    def keep(k):
        return pltpu.make_async_copy(rows_of(k), kept(k), keep_sem.at[k])

    def same_core(body):
        for d in range(2, n, 2):
            body(lax.rem(i + d, n))

    def go_on(z):
        same_core(lambda p: b_copy(p, z).start())

    group = min(n, 256 // q_dev)
    rows = group * q_dev

    def find(at):
        columns = [to_column(p_all[at + b].astype(F32), diag) for b in range(group)]
        target = jnp.concatenate(columns, axis=0).astype(jnp.int32) - i * key_dev
        hits = lax.broadcasted_iota(jnp.int32, (rows, key_dev), 1) == target
        row = jnp.dot(hits.astype(F32).astype(BF16), keys[...], preferred_element_type=F32)
        return target, row

    def work(at, found, start_stats):
        target, row = found
        q = q_all[pl.ds(at, group)].reshape(rows, width)
        slab = keys[...]
        raw = lax.dot_general(q, slab, (((1,), (1,)), ((), ())), preferred_element_type=F32)
        hits = lax.broadcasted_iota(jnp.int32, raw.shape, 1) == target
        top = jnp.max(raw, axis=1, keepdims=True)
        powers = jnp.exp2((raw - top) * (scale * math.log2(math.e)))
        total = jnp.sum(powers, axis=1, keepdims=True)
        others = jnp.where(hits, 0.0, powers).astype(BF16)
        positive = jnp.sum(jnp.where(hits, raw, 0.0), axis=1, keepdims=True)
        for b in range(group):
            span = slice(b * q_dev, (b + 1) * q_dev)
            stat_send[at + b, 0:1] = to_row(top[span], diag) * scale
            stat_send[at + b, 1:2] = to_row(total[span], diag)
            stat_send[at + b, 2:3] = to_row(positive[span], diag) * scale
            stat_send[at + b, 3:4] = jnp.zeros((1, LANES), F32)
        start_stats()
        part = jnp.dot(others, slab, preferred_element_type=F32)
        high = part.astype(BF16)
        low = part - high.astype(F32)
        inside = jnp.logical_and(target >= 0, target < key_dev)
        second = jnp.where(inside, row, low).astype(BF16)
        part_send[pl.ds(at, group), 0] = high.reshape(group, q_dev, width)
        part_send[pl.ds(at, group), 1] = second.reshape(group, q_dev, width)

    def g_copy(p):
        return send(part_send.at[p], part_recv.at[i], g_ss.at[p], g_rs.at[i], (p, j))

    def s_copy(p):
        return send(stat_send.at[p], stat_recv.at[i], s_ss.at[p], s_rs.at[i], (p, j))

    def next_block(z):
        wait_in(block(i, z), z_rs.at[z])
        if by_block:
            go_on(z)

    own_new.wait()
    gy_peers(lambda p: z_copy(p).start())
    gx_peers(lambda p: p_copy(p).start())
    gx_peers(lambda p: q_copy(p).start())
    if by_block:
        go_on(j)
    gy_peers(next_block)
    if not by_block:
        same_core(lambda p: k_copy(p).start())
    f_copy(i).start()
    keep(i).start()
    load_keys.wait()
    gx_peers(lambda p: wait_in(p_all.at[p], p_rs.at[p]))
    whole = n == group
    if whole:
        found = find(0)
    gx_peers(lambda p: wait_in(q_all.at[p], q_rs.at[p]))
    if whole:
        work(0, found, lambda: gx_peers(lambda p: s_copy(p).start()))
    else:
        pl.loop(0, n // group)(lambda c: work(c * group, find(c * group), lambda: None))
        gx_peers(lambda p: s_copy(p).start())
    gx_peers(lambda p: g_copy(p).start())
    part_recv[i] = part_send[i]
    stat_recv[i] = stat_send[i]

    def pass_on(k):
        if by_block:
            for z in range(ngy):
                wait_in(block(k, z), k_rs.at[k * ngy + z])
        else:
            wait_in(rows_of(k), k_rs.at[k])
        f_copy(k).start()
        keep(k).start()

    same_core(pass_on)

    gx_peers(lambda p: wait_in(stat_recv.at[p], s_rs.at[p]))
    top = stat_recv[0, 0:1]
    for s in range(1, n):
        top = jnp.maximum(top, stat_recv[s, 0:1])
    total = jnp.zeros_like(top)
    positive = jnp.zeros_like(top)
    for s in range(n):
        total = total + stat_recv[s, 1:2] * jnp.exp(stat_recv[s, 0:1] - top)
        positive = positive + stat_recv[s, 2:3]
    lse = top + jnp.log(total)
    loss_ref[...] = lse - positive
    own = to_column(p_all[i].astype(F32), diag).astype(jnp.int32)
    at_positive = to_column(jnp.exp(positive - lse) - 1.0, diag)
    factors = [to_column(jnp.exp(stat_recv[s, 0:1] - lse), diag) for s in range(n)]

    gx_peers(lambda p: wait_in(part_recv.at[p], g_rs.at[p]))
    grad = jnp.zeros((q_dev, width), F32)
    for s in range(n):
        first = part_recv[s, 0].astype(F32)
        second = part_recv[s, 1].astype(F32)
        inside = jnp.logical_and(own >= s * key_dev, own < (s + 1) * key_dev)
        grad = grad + factors[s] * first + jnp.where(inside, at_positive, factors[s]) * second
    grad_ref[...] = (grad * scale).astype(BF16)

    loss_store = pltpu.make_async_copy(loss_ref, loss_out, result_sem.at[0])
    grad_store = pltpu.make_async_copy(grad_ref, grad_out, result_sem.at[1])
    loss_store.start()
    grad_store.start()

    def end_sends(p):
        p_copy(p).wait_send()
        q_copy(p).wait_send()
        s_copy(p).wait_send()
        g_copy(p).wait_send()

    gx_peers(end_sends)
    gy_peers(lambda p: z_copy(p).wait_send())
    if by_block:
        for z in range(ngy):
            same_core(lambda p: b_copy(p, z).wait_send())
    else:
        same_core(lambda p: k_copy(p).wait_send())
    f_copy(i).wait_send()
    keep(i).wait()
    same_core(lambda k: f_copy(k).wait_send())
    same_core(lambda k: keep(k).wait())
    for d in range(0, n, 2):
        k = lax.rem(partner + d, n)
        wait_in(kept(k), f_rs.at[k])
    loss_store.wait()
    grad_store.wait()


def finish(
    n, step_ref, loss_ref, grad_ref, queue_ref, arrived_ref, loss_out, grad_out, updated_ref,
    loss_v, loss_w, grad_v, slab, in_sem, out_sem, small_in, small_out,
):
    here = lax.rem(step_ref[0], n) == lax.axis_index("gx")
    pieces = in_sem.shape[0]
    size = slab.shape[0] // pieces

    def part(c):
        return pl.ds(c * size, size)

    def load(src, c):
        return pltpu.make_async_copy(src.at[part(c)], slab.at[part(c)], in_sem.at[c])

    def store(c):
        return pltpu.make_async_copy(slab.at[part(c)], updated_ref.at[part(c)], out_sem.at[c])

    @pl.when(here)
    def _():
        for c in range(pieces):
            load(arrived_ref, c).start()

    @pl.when(jnp.logical_not(here))
    def _():
        for c in range(pieces):
            load(queue_ref, c).start()

    loss_load = pltpu.make_async_copy(loss_ref, loss_v, small_in.at[0])
    grad_load = pltpu.make_async_copy(grad_ref, grad_v, small_in.at[1])
    loss_store = pltpu.make_async_copy(loss_w, loss_out, small_out.at[0])
    grad_store = pltpu.make_async_copy(grad_v, grad_out, small_out.at[1])
    loss_load.start()
    grad_load.start()
    for c in range(pieces):
        load(queue_ref, c).wait()
        store(c).start()
    loss_load.wait()
    loss_w[...] = loss_v[0, 0 : loss_w.shape[0]]
    loss_store.start()
    grad_load.wait()
    grad_store.start()
    for c in range(pieces):
        store(c).wait()
    loss_store.wait()
    grad_store.wait()


def local(n, ngy, queries, positions, queue, new_keys, step):
    q_dev, width = queries.shape
    key_dev = queue.shape[0]
    nk_dev = new_keys.shape[0]
    scale = 2.0 / math.sqrt(width)
    anywhere = pl.BlockSpec(memory_space=pl.ANY)
    dma = pltpu.SemaphoreType.DMA
    rows = n * q_dev
    loss_row, grad, arrived = pl.pallas_call(
        functools.partial(exchange, n, ngy, scale),
        out_shape=(
            jax.ShapeDtypeStruct((1, LANES), F32),
            jax.ShapeDtypeStruct((q_dev, width), BF16),
            jax.ShapeDtypeStruct((n * ngy, nk_dev, width), BF16),
        ),
        in_specs=[anywhere] * 4,
        out_specs=(anywhere,) * 3,
        scratch_shapes=[
            pltpu.VMEM((1, LANES), F32),
            pltpu.VMEM((q_dev, width), BF16),
            dma((2,)),
            pltpu.VMEM((n * ngy, nk_dev, width), BF16),
            dma((n,)),
            pltpu.VMEM((key_dev, width), BF16),
            pltpu.VMEM((n, q_dev, width), BF16),
            pltpu.VMEM((n, 1, LANES), jnp.int32),
            pltpu.VMEM((q_dev,), jnp.int32),
            pltpu.VMEM((n, 2, q_dev, width), BF16),
            pltpu.VMEM((n, 2, q_dev, width), BF16),
            pltpu.VMEM((n, 4, LANES), F32),
            pltpu.VMEM((n, 4, LANES), F32),
            dma((4,)),
            dma((n,)), dma((n,)), dma((n,)), dma((n,)),
            dma((ngy,)), dma((ngy,)),
            dma((n * ngy,)), dma((n * ngy,)), dma((n,)), dma((n,)),
            dma((n,)), dma((n,)), dma((n,)), dma((n,)),
        ],
        compiler_params=pltpu.CompilerParams(
            collective_id=0, has_side_effects=True, vmem_limit_bytes=62 * 2**20
        ),
        cost_estimate=pl.CostEstimate(
            flops=6 * rows * key_dev * width,
            bytes_accessed=2 * key_dev * width * 2,
            transcendentals=rows * key_dev,
        ),
        name="exchange",
    )(queries, positions, queue, new_keys)
    return pl.pallas_call(
        functools.partial(finish, n),
        out_shape=(
            jax.ShapeDtypeStruct((q_dev,), F32),
            jax.ShapeDtypeStruct((q_dev, width), BF16),
            jax.ShapeDtypeStruct((key_dev, width), BF16),
        ),
        in_specs=[pl.BlockSpec(memory_space=pltpu.SMEM)] + [anywhere] * 4,
        out_specs=(anywhere,) * 3,
        scratch_shapes=[
            pltpu.VMEM((1, LANES), F32),
            pltpu.VMEM((q_dev,), F32),
            pltpu.VMEM((q_dev, width), BF16),
            pltpu.VMEM((key_dev, width), BF16),
            dma((8,)),
            dma((8,)),
            dma((2,)),
            dma((2,)),
        ],
        compiler_params=pltpu.CompilerParams(vmem_limit_bytes=62 * 2**20),
        name="finish",
    )(step, loss_row, grad, queue, arrived.reshape(key_dev, width))


def solution(mesh):
    return jax.shard_map(
        functools.partial(local, mesh.shape["gx"], mesh.shape["gy"]),
        mesh=mesh,
        in_specs=(
            P(("gx", "gy"), None),
            P(("gx", "gy")),
            P("gx", None),
            P(("gx", "gy"), None),
            P(),
        ),
        out_specs=(P(("gx", "gy")), P(("gx", "gy"), None), P("gx", None)),
        check_vma=False,
    )
```

```python
import functools
import math

import jax
import jax.numpy as jnp
from jax import lax
from jax.experimental import pallas as pl
from jax.experimental.pallas import tpu as pltpu
from jax.sharding import PartitionSpec as P

MESH = pl.DeviceIdType.MESH
LANES = 128
F32 = jnp.float32
BF16 = jnp.bfloat16


def diagonal(rows):
    shape = (rows, LANES)
    return lax.broadcasted_iota(jnp.int32, shape, 0) == lax.broadcasted_iota(jnp.int32, shape, 1)


def to_column(row, diag):
    return jnp.sum(jnp.where(diag, row, 0.0), axis=1, keepdims=True)


def to_row(column, diag):
    return jnp.sum(jnp.where(diag, column, 0.0), axis=0, keepdims=True)


def exchange(
    n, ngy, scale,
    q_ref, pos_ref, queue_ref, nk_ref,
    loss_out, grad_out, gathered_ref,
    loss_ref, grad_ref, result_sem, arrived_ref, keep_sem, keys, q_all, p_all, pos_v, part_send, part_recv, stat_send, stat_recv,
    local_sem, q_ss, q_rs, p_ss, p_rs, z_ss, z_rs, k_ss, k_rs, f_ss, f_rs, g_ss, g_rs, s_ss, s_rs,
):
    i = lax.axis_index("gx")
    j = lax.axis_index("gy")
    q_dev, width = q_ref.shape
    key_dev = queue_ref.shape[0]

    def send(src, dst, ss, rs, to):
        return pltpu.make_async_remote_copy(
            src_ref=src, dst_ref=dst, send_sem=ss, recv_sem=rs, device_id=to, device_id_type=MESH
        )

    def gx_peers(body):
        for d in range(1, n):
            body(lax.rem(i + d, n))

    def gy_peers(body):
        turn = 1 - 2 * ((2 * j) // ngy)
        for d in range(1, ngy):
            body(lax.rem(j + turn * d + ngy, ngy))

    load_pos = pltpu.make_async_copy(pos_ref, pos_v, local_sem.at[0])
    load_q = pltpu.make_async_copy(q_ref, q_all.at[i], local_sem.at[1])
    load_keys = pltpu.make_async_copy(queue_ref, keys, local_sem.at[2])
    own_new = pltpu.make_async_copy(nk_ref, arrived_ref.at[i * ngy + j], local_sem.at[3])
    load_pos.start()
    load_q.start()
    load_keys.start()
    own_new.start()

    barrier = pltpu.get_barrier_semaphore()
    gx_peers(lambda p: pl.semaphore_signal(barrier, inc=1, device_id=(p, j), device_id_type=MESH))
    gy_peers(lambda p: pl.semaphore_signal(barrier, inc=1, device_id=(i, p), device_id_type=MESH))
    load_pos.wait()
    load_q.wait()
    diag = diagonal(q_dev)
    p_all[i] = jnp.zeros((1, LANES), jnp.int32)
    p_all[i, :, 0:q_dev] = pos_v[...].reshape(1, q_dev)
    pl.semaphore_wait(barrier, n + ngy - 2)

    def q_copy(p):
        return send(q_all.at[i], q_all.at[i], q_ss.at[p], q_rs.at[i], (p, j))

    def p_copy(p):
        return send(p_all.at[i], p_all.at[i], p_ss.at[p], p_rs.at[i], (p, j))

    by_block = n * ngy <= 32
    core = lax.rem(i, 2)
    partner = i + 1 - 2 * core

    def wait_in(dst, sem):
        pltpu.make_async_copy(dst, dst, sem).wait()

    def block(k, z):
        return arrived_ref.at[k * ngy + z]

    def rows_of(k):
        return arrived_ref.at[pl.ds(k * ngy, ngy)]

    def z_copy(p):
        return send(block(i, j), block(i, j), z_ss.at[p], z_rs.at[j], (i, p))

    def b_copy(p, z):
        return send(block(i, z), block(i, z), k_ss.at[p * ngy + z], k_rs.at[i * ngy + z], (p, j))

    def k_copy(p):
        return send(rows_of(i), rows_of(i), k_ss.at[p], k_rs.at[i], (p, j))

    def kept(k):
        return gathered_ref.at[pl.ds(k * ngy, ngy)]

    def f_copy(k):
        return send(rows_of(k), kept(k), f_ss.at[k], f_rs.at[k], (partner, j))

    def keep(k):
        return pltpu.make_async_copy(rows_of(k), kept(k), keep_sem.at[k])

    def same_core(body):
        for d in range(2, n, 2):
            body(lax.rem(i + d, n))

    def go_on(z):
        same_core(lambda p: b_copy(p, z).start())

    group = min(n, 256 // q_dev)
    rows = group * q_dev

    def find(at):
        columns = [to_column(p_all[at + b].astype(F32), diag) for b in range(group)]
        target = jnp.concatenate(columns, axis=0).astype(jnp.int32) - i * key_dev
        return target

    def work(at, target, start_stats):
        q = q_all[pl.ds(at, group)].reshape(rows, width)
        slab = keys[...]
        raw = lax.dot_general(q, slab, (((1,), (1,)), ((), ())), preferred_element_type=F32)
        hits = lax.broadcasted_iota(jnp.int32, raw.shape, 1) == target
        top = jnp.max(raw, axis=1, keepdims=True)
        powers = jnp.exp2((raw - top) * (scale * math.log2(math.e)))
        total = jnp.sum(powers, axis=1, keepdims=True)
        others = jnp.where(hits, 0.0, powers).astype(BF16)
        positive = jnp.sum(jnp.where(hits, raw, 0.0), axis=1, keepdims=True)
        for b in range(group):
            span = slice(b * q_dev, (b + 1) * q_dev)
            stat_send[at + b, 0:1] = to_row(top[span], diag) * scale
            stat_send[at + b, 1:2] = to_row(total[span], diag)
            stat_send[at + b, 2:3] = to_row(positive[span], diag) * scale
            stat_send[at + b, 3:4] = jnp.zeros((1, LANES), F32)
        start_stats()
        stacked = jnp.concatenate([others, jnp.where(hits, 1.0, 0.0).astype(BF16)], axis=0)
        both = jnp.dot(stacked, slab, preferred_element_type=F32)
        part, row = both[:rows], both[rows:]
        high = part.astype(BF16)
        low = part - high.astype(F32)
        inside = jnp.logical_and(target >= 0, target < key_dev)
        second = jnp.where(inside, row, low).astype(BF16)
        part_send[pl.ds(at, group), 0] = high.reshape(group, q_dev, width)
        part_send[pl.ds(at, group), 1] = second.reshape(group, q_dev, width)

    def g_copy(p):
        return send(part_send.at[p], part_recv.at[i], g_ss.at[p], g_rs.at[i], (p, j))

    def s_copy(p):
        return send(stat_send.at[p], stat_recv.at[i], s_ss.at[p], s_rs.at[i], (p, j))

    def next_block(z):
        wait_in(block(i, z), z_rs.at[z])
        if by_block:
            go_on(z)

    own_new.wait()
    gy_peers(lambda p: z_copy(p).start())
    gx_peers(lambda p: p_copy(p).start())
    gx_peers(lambda p: q_copy(p).start())
    if by_block:
        go_on(j)
    gy_peers(next_block)
    if not by_block:
        same_core(lambda p: k_copy(p).start())
    f_copy(i).start()
    keep(i).start()
    load_keys.wait()
    gx_peers(lambda p: wait_in(p_all.at[p], p_rs.at[p]))
    whole = n == group
    if whole:
        found = find(0)
    gx_peers(lambda p: wait_in(q_all.at[p], q_rs.at[p]))
    if whole:
        work(0, found, lambda: gx_peers(lambda p: s_copy(p).start()))
    else:
        pl.loop(0, n // group)(lambda c: work(c * group, find(c * group), lambda: None))
        gx_peers(lambda p: s_copy(p).start())
    gx_peers(lambda p: g_copy(p).start())
    part_recv[i] = part_send[i]
    stat_recv[i] = stat_send[i]

    def pass_on(k):
        if by_block:
            for z in range(ngy):
                wait_in(block(k, z), k_rs.at[k * ngy + z])
        else:
            wait_in(rows_of(k), k_rs.at[k])
        f_copy(k).start()
        keep(k).start()

    same_core(pass_on)

    gx_peers(lambda p: wait_in(stat_recv.at[p], s_rs.at[p]))
    top = stat_recv[0, 0:1]
    for s in range(1, n):
        top = jnp.maximum(top, stat_recv[s, 0:1])
    total = jnp.zeros_like(top)
    positive = jnp.zeros_like(top)
    for s in range(n):
        total = total + stat_recv[s, 1:2] * jnp.exp(stat_recv[s, 0:1] - top)
        positive = positive + stat_recv[s, 2:3]
    lse = top + jnp.log(total)
    loss_ref[...] = lse - positive
    own = to_column(p_all[i].astype(F32), diag).astype(jnp.int32)
    at_positive = to_column(jnp.exp(positive - lse) - 1.0, diag)
    factors = [to_column(jnp.exp(stat_recv[s, 0:1] - lse), diag) for s in range(n)]

    gx_peers(lambda p: wait_in(part_recv.at[p], g_rs.at[p]))
    grad = jnp.zeros((q_dev, width), F32)
    for s in range(n):
        first = part_recv[s, 0].astype(F32)
        second = part_recv[s, 1].astype(F32)
        inside = jnp.logical_and(own >= s * key_dev, own < (s + 1) * key_dev)
        grad = grad + factors[s] * first + jnp.where(inside, at_positive, factors[s]) * second
    grad_ref[...] = (grad * scale).astype(BF16)

    loss_store = pltpu.make_async_copy(loss_ref, loss_out, result_sem.at[0])
    grad_store = pltpu.make_async_copy(grad_ref, grad_out, result_sem.at[1])
    loss_store.start()
    grad_store.start()

    def end_sends(p):
        p_copy(p).wait_send()
        q_copy(p).wait_send()
        s_copy(p).wait_send()
        g_copy(p).wait_send()

    gx_peers(end_sends)
    gy_peers(lambda p: z_copy(p).wait_send())
    if by_block:
        for z in range(ngy):
            same_core(lambda p: b_copy(p, z).wait_send())
    else:
        same_core(lambda p: k_copy(p).wait_send())
    f_copy(i).wait_send()
    keep(i).wait()
    same_core(lambda k: f_copy(k).wait_send())
    same_core(lambda k: keep(k).wait())
    for d in range(0, n, 2):
        k = lax.rem(partner + d, n)
        wait_in(kept(k), f_rs.at[k])
    loss_store.wait()
    grad_store.wait()


def finish(
    n, step_ref, loss_ref, grad_ref, queue_ref, arrived_ref, loss_out, grad_out, updated_ref,
    loss_v, loss_w, grad_v, slab, in_sem, out_sem, small_in, small_out,
):
    here = lax.rem(step_ref[0], n) == lax.axis_index("gx")
    pieces = in_sem.shape[0]
    size = slab.shape[0] // pieces

    def part(c):
        return pl.ds(c * size, size)

    def load(src, c):
        return pltpu.make_async_copy(src.at[part(c)], slab.at[part(c)], in_sem.at[c])

    def store(c):
        return pltpu.make_async_copy(slab.at[part(c)], updated_ref.at[part(c)], out_sem.at[c])

    @pl.when(here)
    def _():
        for c in range(pieces):
            load(arrived_ref, c).start()

    @pl.when(jnp.logical_not(here))
    def _():
        for c in range(pieces):
            load(queue_ref, c).start()

    loss_load = pltpu.make_async_copy(loss_ref, loss_v, small_in.at[0])
    grad_load = pltpu.make_async_copy(grad_ref, grad_v, small_in.at[1])
    loss_store = pltpu.make_async_copy(loss_w, loss_out, small_out.at[0])
    grad_store = pltpu.make_async_copy(grad_v, grad_out, small_out.at[1])
    loss_load.start()
    grad_load.start()
    for c in range(pieces):
        load(queue_ref, c).wait()
        store(c).start()
    loss_load.wait()
    loss_w[...] = loss_v[0, 0 : loss_w.shape[0]]
    loss_store.start()
    grad_load.wait()
    grad_store.start()
    for c in range(pieces):
        store(c).wait()
    loss_store.wait()
    grad_store.wait()


def local(n, ngy, queries, positions, queue, new_keys, step):
    q_dev, width = queries.shape
    key_dev = queue.shape[0]
    nk_dev = new_keys.shape[0]
    scale = 2.0 / math.sqrt(width)
    anywhere = pl.BlockSpec(memory_space=pl.ANY)
    dma = pltpu.SemaphoreType.DMA
    rows = n * q_dev
    loss_row, grad, arrived = pl.pallas_call(
        functools.partial(exchange, n, ngy, scale),
        out_shape=(
            jax.ShapeDtypeStruct((1, LANES), F32),
            jax.ShapeDtypeStruct((q_dev, width), BF16),
            jax.ShapeDtypeStruct((n * ngy, nk_dev, width), BF16),
        ),
        in_specs=[anywhere] * 4,
        out_specs=(anywhere,) * 3,
        scratch_shapes=[
            pltpu.VMEM((1, LANES), F32),
            pltpu.VMEM((q_dev, width), BF16),
            dma((2,)),
            pltpu.VMEM((n * ngy, nk_dev, width), BF16),
            dma((n,)),
            pltpu.VMEM((key_dev, width), BF16),
            pltpu.VMEM((n, q_dev, width), BF16),
            pltpu.VMEM((n, 1, LANES), jnp.int32),
            pltpu.VMEM((q_dev,), jnp.int32),
            pltpu.VMEM((n, 2, q_dev, width), BF16),
            pltpu.VMEM((n, 2, q_dev, width), BF16),
            pltpu.VMEM((n, 4, LANES), F32),
            pltpu.VMEM((n, 4, LANES), F32),
            dma((4,)),
            dma((n,)), dma((n,)), dma((n,)), dma((n,)),
            dma((ngy,)), dma((ngy,)),
            dma((n * ngy,)), dma((n * ngy,)), dma((n,)), dma((n,)),
            dma((n,)), dma((n,)), dma((n,)), dma((n,)),
        ],
        compiler_params=pltpu.CompilerParams(
            collective_id=0, has_side_effects=True, vmem_limit_bytes=62 * 2**20
        ),
        cost_estimate=pl.CostEstimate(
            flops=6 * rows * key_dev * width,
            bytes_accessed=2 * key_dev * width * 2,
            transcendentals=rows * key_dev,
        ),
        name="exchange",
    )(queries, positions, queue, new_keys)
    return pl.pallas_call(
        functools.partial(finish, n),
        out_shape=(
            jax.ShapeDtypeStruct((q_dev,), F32),
            jax.ShapeDtypeStruct((q_dev, width), BF16),
            jax.ShapeDtypeStruct((key_dev, width), BF16),
        ),
        in_specs=[pl.BlockSpec(memory_space=pltpu.SMEM)] + [anywhere] * 4,
        out_specs=(anywhere,) * 3,
        scratch_shapes=[
            pltpu.VMEM((1, LANES), F32),
            pltpu.VMEM((q_dev,), F32),
            pltpu.VMEM((q_dev, width), BF16),
            pltpu.VMEM((key_dev, width), BF16),
            dma((8,)),
            dma((8,)),
            dma((2,)),
            dma((2,)),
        ],
        compiler_params=pltpu.CompilerParams(vmem_limit_bytes=62 * 2**20),
        name="finish",
    )(step, loss_row, grad, queue, arrived.reshape(key_dev, width))


def solution(mesh):
    return jax.shard_map(
        functools.partial(local, mesh.shape["gx"], mesh.shape["gy"]),
        mesh=mesh,
        in_specs=(
            P(("gx", "gy"), None),
            P(("gx", "gy")),
            P("gx", None),
            P(("gx", "gy"), None),
            P(),
        ),
        out_specs=(P(("gx", "gy")), P(("gx", "gy"), None), P("gx", None)),
        check_vma=False,
    )
```

```python
import functools
import math

import jax
import jax.numpy as jnp
from jax import lax
from jax.experimental import pallas as pl
from jax.experimental.pallas import tpu as pltpu
from jax.sharding import PartitionSpec as P

MESH = pl.DeviceIdType.MESH
LANES = 128
F32 = jnp.float32
BF16 = jnp.bfloat16


def diagonal(rows):
    shape = (rows, LANES)
    return lax.broadcasted_iota(jnp.int32, shape, 0) == lax.broadcasted_iota(jnp.int32, shape, 1)


def to_column(row, diag):
    return jnp.sum(jnp.where(diag, row, 0.0), axis=1, keepdims=True)


def to_row(column, diag):
    return jnp.sum(jnp.where(diag, column, 0.0), axis=0, keepdims=True)


def exchange(
    n, ngy, scale,
    q_ref, pos_ref, queue_ref, nk_ref,
    loss_out, grad_out, gathered_ref,
    loss_ref, grad_ref, result_sem, arrived_ref, keep_sem, keys, q_all, p_all, pos_v, part_send, part_recv, stat_send, stat_recv,
    local_sem, q_ss, q_rs, p_ss, p_rs, z_ss, z_rs, k_ss, k_rs, f_ss, f_rs, g_ss, g_rs, s_ss, s_rs,
):
    i = lax.axis_index("gx")
    j = lax.axis_index("gy")
    q_dev, width = q_ref.shape
    key_dev = queue_ref.shape[0]

    def send(src, dst, ss, rs, to):
        return pltpu.make_async_remote_copy(
            src_ref=src, dst_ref=dst, send_sem=ss, recv_sem=rs, device_id=to, device_id_type=MESH
        )

    def gx_peers(body):
        for d in range(1, n):
            body(lax.rem(i + d, n))

    def gy_peers(body):
        turn = 1 - 2 * ((2 * j) // ngy)
        for d in range(1, ngy):
            body(lax.rem(j + turn * d + ngy, ngy))

    load_pos = pltpu.make_async_copy(pos_ref, pos_v, local_sem.at[0])
    load_q = pltpu.make_async_copy(q_ref, q_all.at[i], local_sem.at[1])
    load_keys = pltpu.make_async_copy(queue_ref, keys, local_sem.at[2])
    own_new = pltpu.make_async_copy(nk_ref, arrived_ref.at[i * ngy + j], local_sem.at[3])
    load_pos.start()
    load_q.start()
    load_keys.start()
    own_new.start()

    barrier = pltpu.get_barrier_semaphore()
    gx_peers(lambda p: pl.semaphore_signal(barrier, inc=1, device_id=(p, j), device_id_type=MESH))
    gy_peers(lambda p: pl.semaphore_signal(barrier, inc=1, device_id=(i, p), device_id_type=MESH))
    load_pos.wait()
    load_q.wait()
    diag = diagonal(q_dev)
    p_all[i] = jnp.zeros((1, LANES), jnp.int32)
    p_all[i, :, 0:q_dev] = pos_v[...].reshape(1, q_dev)
    pl.semaphore_wait(barrier, n + ngy - 2)

    def q_copy(p):
        return send(q_all.at[i], q_all.at[i], q_ss.at[p], q_rs.at[i], (p, j))

    def p_copy(p):
        return send(p_all.at[i], p_all.at[i], p_ss.at[p], p_rs.at[i], (p, j))

    by_block = n * ngy <= 32
    core = lax.rem(i, 2)
    partner = i + 1 - 2 * core

    def wait_in(dst, sem):
        pltpu.make_async_copy(dst, dst, sem).wait()

    def block(k, z):
        return arrived_ref.at[k * ngy + z]

    def rows_of(k):
        return arrived_ref.at[pl.ds(k * ngy, ngy)]

    def z_copy(p):
        return send(block(i, j), block(i, j), z_ss.at[p], z_rs.at[j], (i, p))

    def b_copy(p, z):
        return send(block(i, z), block(i, z), k_ss.at[p * ngy + z], k_rs.at[i * ngy + z], (p, j))

    def k_copy(p):
        return send(rows_of(i), rows_of(i), k_ss.at[p], k_rs.at[i], (p, j))

    def kept(k):
        return gathered_ref.at[pl.ds(k * ngy, ngy)]

    def f_copy(k):
        return send(rows_of(k), kept(k), f_ss.at[k], f_rs.at[k], (partner, j))

    def keep(k):
        return pltpu.make_async_copy(rows_of(k), kept(k), keep_sem.at[k])

    def same_core(body):
        for d in range(2, n, 2):
            body(lax.rem(i + d, n))

    def go_on(z):
        same_core(lambda p: b_copy(p, z).start())

    group = n // 2 if by_block else min(n, 256 // q_dev)
    rows = group * q_dev

    def find(at):
        columns = [to_column(p_all[at + b].astype(F32), diag) for b in range(group)]
        target = jnp.concatenate(columns, axis=0).astype(jnp.int32) - i * key_dev
        hits = lax.broadcasted_iota(jnp.int32, (rows, key_dev), 1) == target
        row = jnp.dot(hits.astype(F32).astype(BF16), keys[...], preferred_element_type=F32)
        return target, row

    def work(at, found, start_stats):
        target, row = found
        q = q_all[pl.ds(at, group)].reshape(rows, width)
        slab = keys[...]
        raw = lax.dot_general(q, slab, (((1,), (1,)), ((), ())), preferred_element_type=F32)
        hits = lax.broadcasted_iota(jnp.int32, raw.shape, 1) == target
        top = jnp.max(raw, axis=1, keepdims=True)
        powers = jnp.exp2((raw - top) * (scale * math.log2(math.e)))
        total = jnp.sum(powers, axis=1, keepdims=True)
        others = jnp.where(hits, 0.0, powers).astype(BF16)
        positive = jnp.sum(jnp.where(hits, raw, 0.0), axis=1, keepdims=True)
        for b in range(group):
            span = slice(b * q_dev, (b + 1) * q_dev)
            stat_send[at + b, 0:1] = to_row(top[span], diag) * scale
            stat_send[at + b, 1:2] = to_row(total[span], diag)
            stat_send[at + b, 2:3] = to_row(positive[span], diag) * scale
            stat_send[at + b, 3:4] = jnp.zeros((1, LANES), F32)
        start_stats()
        part = jnp.dot(others, slab, preferred_element_type=F32)
        high = part.astype(BF16)
        low = part - high.astype(F32)
        inside = jnp.logical_and(target >= 0, target < key_dev)
        second = jnp.where(inside, row, low).astype(BF16)
        part_send[pl.ds(at, group), 0] = high.reshape(group, q_dev, width)
        part_send[pl.ds(at, group), 1] = second.reshape(group, q_dev, width)

    def g_copy(p):
        return send(part_send.at[p], part_recv.at[i], g_ss.at[p], g_rs.at[i], (p, j))

    def s_copy(p):
        return send(stat_send.at[p], stat_recv.at[i], s_ss.at[p], s_rs.at[i], (p, j))

    def next_block(z):
        wait_in(block(i, z), z_rs.at[z])
        if by_block:
            go_on(z)

    own_new.wait()
    gy_peers(lambda p: z_copy(p).start())
    gx_peers(lambda p: p_copy(p).start())
    gx_peers(lambda p: q_copy(p).start())
    if by_block:
        go_on(j)
    gy_peers(next_block)
    if not by_block:
        same_core(lambda p: k_copy(p).start())
    f_copy(i).start()
    keep(i).start()
    load_keys.wait()
    gx_peers(lambda p: wait_in(p_all.at[p], p_rs.at[p]))
    if by_block:
        near = (i // group) * group
        far = n - group - near
        halves = (
            (far, [far + b for b in range(group)]),
            (near, [near + lax.rem(i - near + d, group) for d in range(1, group)]),
        )
        for at, peers in halves:
            found = find(at)
            for p in peers:
                wait_in(q_all.at[p], q_rs.at[p])
            work(at, found, lambda: [s_copy(p).start() for p in peers])
            for p in peers:
                g_copy(p).start()
    else:
        gx_peers(lambda p: wait_in(q_all.at[p], q_rs.at[p]))
        pl.loop(0, n // group)(lambda c: work(c * group, find(c * group), lambda: None))
        gx_peers(lambda p: s_copy(p).start())
        gx_peers(lambda p: g_copy(p).start())
    part_recv[i] = part_send[i]
    stat_recv[i] = stat_send[i]

    def pass_on(k):
        if by_block:
            for z in range(ngy):
                wait_in(block(k, z), k_rs.at[k * ngy + z])
        else:
            wait_in(rows_of(k), k_rs.at[k])
        f_copy(k).start()
        keep(k).start()

    same_core(pass_on)

    gx_peers(lambda p: wait_in(stat_recv.at[p], s_rs.at[p]))
    top = stat_recv[0, 0:1]
    for s in range(1, n):
        top = jnp.maximum(top, stat_recv[s, 0:1])
    total = jnp.zeros_like(top)
    positive = jnp.zeros_like(top)
    for s in range(n):
        total = total + stat_recv[s, 1:2] * jnp.exp(stat_recv[s, 0:1] - top)
        positive = positive + stat_recv[s, 2:3]
    lse = top + jnp.log(total)
    loss_ref[...] = lse - positive
    own = to_column(p_all[i].astype(F32), diag).astype(jnp.int32)
    at_positive = to_column(jnp.exp(positive - lse) - 1.0, diag)
    factors = [to_column(jnp.exp(stat_recv[s, 0:1] - lse), diag) for s in range(n)]

    gx_peers(lambda p: wait_in(part_recv.at[p], g_rs.at[p]))
    grad = jnp.zeros((q_dev, width), F32)
    for s in range(n):
        first = part_recv[s, 0].astype(F32)
        second = part_recv[s, 1].astype(F32)
        inside = jnp.logical_and(own >= s * key_dev, own < (s + 1) * key_dev)
        grad = grad + factors[s] * first + jnp.where(inside, at_positive, factors[s]) * second
    grad_ref[...] = (grad * scale).astype(BF16)

    loss_store = pltpu.make_async_copy(loss_ref, loss_out, result_sem.at[0])
    grad_store = pltpu.make_async_copy(grad_ref, grad_out, result_sem.at[1])
    loss_store.start()
    grad_store.start()

    def end_sends(p):
        p_copy(p).wait_send()
        q_copy(p).wait_send()
        s_copy(p).wait_send()
        g_copy(p).wait_send()

    gx_peers(end_sends)
    gy_peers(lambda p: z_copy(p).wait_send())
    if by_block:
        for z in range(ngy):
            same_core(lambda p: b_copy(p, z).wait_send())
    else:
        same_core(lambda p: k_copy(p).wait_send())
    f_copy(i).wait_send()
    keep(i).wait()
    same_core(lambda k: f_copy(k).wait_send())
    same_core(lambda k: keep(k).wait())
    for d in range(0, n, 2):
        k = lax.rem(partner + d, n)
        wait_in(kept(k), f_rs.at[k])
    loss_store.wait()
    grad_store.wait()


def finish(
    n, step_ref, loss_ref, grad_ref, queue_ref, arrived_ref, loss_out, grad_out, updated_ref,
    loss_v, loss_w, grad_v, slab, in_sem, out_sem, small_in, small_out,
):
    here = lax.rem(step_ref[0], n) == lax.axis_index("gx")
    pieces = in_sem.shape[0]
    size = slab.shape[0] // pieces

    def part(c):
        return pl.ds(c * size, size)

    def load(src, c):
        return pltpu.make_async_copy(src.at[part(c)], slab.at[part(c)], in_sem.at[c])

    def store(c):
        return pltpu.make_async_copy(slab.at[part(c)], updated_ref.at[part(c)], out_sem.at[c])

    @pl.when(here)
    def _():
        for c in range(pieces):
            load(arrived_ref, c).start()

    @pl.when(jnp.logical_not(here))
    def _():
        for c in range(pieces):
            load(queue_ref, c).start()

    loss_load = pltpu.make_async_copy(loss_ref, loss_v, small_in.at[0])
    grad_load = pltpu.make_async_copy(grad_ref, grad_v, small_in.at[1])
    loss_store = pltpu.make_async_copy(loss_w, loss_out, small_out.at[0])
    grad_store = pltpu.make_async_copy(grad_v, grad_out, small_out.at[1])
    loss_load.start()
    grad_load.start()
    for c in range(pieces):
        load(queue_ref, c).wait()
        store(c).start()
    loss_load.wait()
    loss_w[...] = loss_v[0, 0 : loss_w.shape[0]]
    loss_store.start()
    grad_load.wait()
    grad_store.start()
    for c in range(pieces):
        store(c).wait()
    loss_store.wait()
    grad_store.wait()


def local(n, ngy, queries, positions, queue, new_keys, step):
    q_dev, width = queries.shape
    key_dev = queue.shape[0]
    nk_dev = new_keys.shape[0]
    scale = 2.0 / math.sqrt(width)
    anywhere = pl.BlockSpec(memory_space=pl.ANY)
    dma = pltpu.SemaphoreType.DMA
    rows = n * q_dev
    loss_row, grad, arrived = pl.pallas_call(
        functools.partial(exchange, n, ngy, scale),
        out_shape=(
            jax.ShapeDtypeStruct((1, LANES), F32),
            jax.ShapeDtypeStruct((q_dev, width), BF16),
            jax.ShapeDtypeStruct((n * ngy, nk_dev, width), BF16),
        ),
        in_specs=[anywhere] * 4,
        out_specs=(anywhere,) * 3,
        scratch_shapes=[
            pltpu.VMEM((1, LANES), F32),
            pltpu.VMEM((q_dev, width), BF16),
            dma((2,)),
            pltpu.VMEM((n * ngy, nk_dev, width), BF16),
            dma((n,)),
            pltpu.VMEM((key_dev, width), BF16),
            pltpu.VMEM((n, q_dev, width), BF16),
            pltpu.VMEM((n, 1, LANES), jnp.int32),
            pltpu.VMEM((q_dev,), jnp.int32),
            pltpu.VMEM((n, 2, q_dev, width), BF16),
            pltpu.VMEM((n, 2, q_dev, width), BF16),
            pltpu.VMEM((n, 4, LANES), F32),
            pltpu.VMEM((n, 4, LANES), F32),
            dma((4,)),
            dma((n,)), dma((n,)), dma((n,)), dma((n,)),
            dma((ngy,)), dma((ngy,)),
            dma((n * ngy,)), dma((n * ngy,)), dma((n,)), dma((n,)),
            dma((n,)), dma((n,)), dma((n,)), dma((n,)),
        ],
        compiler_params=pltpu.CompilerParams(
            collective_id=0, has_side_effects=True, vmem_limit_bytes=62 * 2**20
        ),
        cost_estimate=pl.CostEstimate(
            flops=6 * rows * key_dev * width,
            bytes_accessed=2 * key_dev * width * 2,
            transcendentals=rows * key_dev,
        ),
        name="exchange",
    )(queries, positions, queue, new_keys)
    return pl.pallas_call(
        functools.partial(finish, n),
        out_shape=(
            jax.ShapeDtypeStruct((q_dev,), F32),
            jax.ShapeDtypeStruct((q_dev, width), BF16),
            jax.ShapeDtypeStruct((key_dev, width), BF16),
        ),
        in_specs=[pl.BlockSpec(memory_space=pltpu.SMEM)] + [anywhere] * 4,
        out_specs=(anywhere,) * 3,
        scratch_shapes=[
            pltpu.VMEM((1, LANES), F32),
            pltpu.VMEM((q_dev,), F32),
            pltpu.VMEM((q_dev, width), BF16),
            pltpu.VMEM((key_dev, width), BF16),
            dma((8,)),
            dma((8,)),
            dma((2,)),
            dma((2,)),
        ],
        compiler_params=pltpu.CompilerParams(vmem_limit_bytes=62 * 2**20),
        name="finish",
    )(step, loss_row, grad, queue, arrived.reshape(key_dev, width))


def solution(mesh):
    return jax.shard_map(
        functools.partial(local, mesh.shape["gx"], mesh.shape["gy"]),
        mesh=mesh,
        in_specs=(
            P(("gx", "gy"), None),
            P(("gx", "gy")),
            P("gx", None),
            P(("gx", "gy"), None),
            P(),
        ),
        out_specs=(P(("gx", "gy")), P(("gx", "gy"), None), P("gx", None)),
        check_vma=False,
    )
```
